256 devices in a mesh: dp: 32 (over x, y, core), owner: 8 (over z).
Axes of the slice: x: 4, y: 4, z: 8, core: 2. Of those that a mesh axis runs over, the one named last changes fastest.
Arguments:
- momentum: float32 [192, 1024, 768], P(None, ('dp', 'owner')), may hold values from -6 to 6
- grad: bfloat16 [192, 1024, 768], P(None, ('dp', 'owner'))
- owner_table: int32 [192], replicated, may hold values from 0 to 255, as said below
Outputs:
- new_momentum: float32 [192, 1024, 768], P(None, ('dp', 'owner'))
- update: float32 [192, 1024, 768], P(None, ('dp', 'owner'))
- owned_update: bfloat16 [2, 256, 1024, 768], P(None, ('dp', 'owner'))
The draws below stay inside these ranges and needn't reach their ends.
Inputs may be any that keep to these rules, and one draw needn't show every extreme that they name: `owner_table`: no device owns more than 2 matrices, and some device owns exactly 2.
All inputs are finite; a program needn't handle non-finite values.
Results may differ from the reference program's by a relative error of at most 0.0073.
Values may be sent and summed in bfloat16 or wider, within the bound.
No kernel may reach another device: no remote copies, remote signals or barrier semaphores. Data moves between devices by JAX's collectives and lax.ppermute only.
A program may use at most 64 MiB of HBM per device.

```python
import math
import jax
import jax.numpy as jnp
from jax import lax

R = 1024
C = 768
ITERS = 2
CAP = 2
MATS = 192
N_DP = 32
N_OWNER = 8
DEVICES = 256


def draw_grad(key, part):
    key = jax.random.fold_in(key, 7)
    keys = jax.random.split(key, 3)
    row_scale = jnp.exp(jax.random.uniform(keys[0], (MATS, R, 1), jnp.float32, 0.0, math.log(10.0)))
    col_scale = jnp.exp(jax.random.uniform(keys[1], (MATS, 1, C), jnp.float32, 0.0, math.log(10.0)))
    base = jax.random.normal(keys[2], (MATS, R, C), jnp.float32)
    return (0.1 * base * row_scale * col_scale).astype(jnp.bfloat16)


def draw_owner_table(key, part):
    key = jax.random.fold_in(key, 11)
    keys = jax.random.split(key, 3)
    order = jax.random.permutation(keys[0], DEVICES)
    paired = jax.random.randint(keys[1], (), 1, MATS // 4 + 1)
    index = jnp.arange(MATS)
    owners = jnp.where(index < 2 * paired, order[index // 2], order[jnp.maximum(index - paired, 0)])
    return owners[jax.random.permutation(keys[2], MATS)].astype(jnp.int32)


def block_levels(stream_key, shape, shards, low, largest):
    def one(dim, shards_of):
        steps = jax.random.uniform(jax.random.fold_in(jax.random.fold_in(stream_key, 6), dim), (shards_of,), jnp.float32, low / len(shards), largest / len(shards))
        return jnp.repeat(jnp.exp(steps), shape[dim] // shards_of).reshape((-1,) + (1,) * (len(shape) - dim - 1))

    gain = one(*shards[0])
    for cut in shards[1:]:
        gain = gain * one(*cut)
    return gain


def noise(key, dims, deviation, limit, cuts=(), dtype=jnp.bfloat16):
    array = jax.random.normal(key, dims, jnp.float32) * deviation
    if len(cuts) > 0:
        array = block_levels(key, dims, cuts, -0.22, 0.18) * array
    return jnp.clip(array, min=-limit, max=limit).astype(dtype)


def setup_inputs(seed: int = 0) -> dict:
    key_of = jax.random.split(jax.random.key(seed), 4)
    momentum = noise(key_of[0], (MATS, R, C), 1.0, 6.0, ((1, 256),), jnp.float32)
    grad = draw_grad(jax.random.fold_in(key_of[3], 71), 0)
    owner_table = draw_owner_table(jax.random.fold_in(key_of[3], 71), 0)
    return dict(momentum=momentum, grad=grad, owner_table=owner_table)


momentum_decay = 0.95
quintic_one = 3.4445
quintic_two = -4.775
quintic_three = 2.0315
norm_epsilon = 1e-07

def orthogonalize(matrix):
    values = matrix.astype(jnp.float32)
    frobenius = jnp.sqrt(jnp.sum(values * values))
    iterate = (values / (frobenius + norm_epsilon)).astype(jnp.bfloat16)
    for step in range(ITERS):
        gram = lax.dot_general(iterate, iterate, (((0,), (0,)), ((), ())), preferred_element_type=jnp.float32).astype(jnp.bfloat16)
        square = jnp.dot(gram, gram, preferred_element_type=jnp.float32)
        poly = (quintic_two * gram.astype(jnp.float32) + quintic_three * square).astype(jnp.bfloat16)
        iterate = (quintic_one * iterate.astype(jnp.float32) + jnp.dot(iterate, poly, preferred_element_type=jnp.float32)).astype(jnp.bfloat16)
    return iterate

def owner_rank(owner_table):
    total_mats = owner_table.shape[0]
    matching = owner_table[:, None] == owner_table[None, :]
    earlier = lax.broadcasted_iota(jnp.int32, (total_mats, total_mats), 1) < lax.broadcasted_iota(jnp.int32, (total_mats, total_mats), 0)
    return lax.optimization_barrier(jnp.sum(jnp.logical_and(matching, earlier).astype(jnp.int32), axis=1)).astype(jnp.int32)

def reference(momentum, grad, owner_table):
    grad_values = grad.astype(jnp.float32)
    new_momentum = momentum_decay * momentum + grad_values
    nesterov = (grad_values + momentum_decay * new_momentum).astype(jnp.bfloat16)
    iterates = lax.map(orthogonalize, nesterov)
    update = math.sqrt(R) * iterates.astype(jnp.float32)
    rank = owner_rank(owner_table)
    owned_update = jnp.zeros((CAP, N_DP * N_OWNER, R, C), jnp.bfloat16).at[rank, owner_table].set(update.astype(jnp.bfloat16))
    return (new_momentum, update, owned_update)
```

```python
import functools
import math

import jax
import jax.numpy as jnp
from jax import lax
from jax.experimental import pallas as pl
from jax.experimental.pallas import tpu as pltpu
from jax.sharding import PartitionSpec as P

ITERS = 2
CAP = 2

momentum_decay = 0.95
quintic_one = 3.4445
quintic_two = -4.775
quintic_three = 2.0315
norm_epsilon = 1e-07

SLOT, HELPER, FIRST, SECOND, SPILLED = range(5)
TABLE_ROWS = 8


def table_kernel(planes, owner_ref, table_ref):
    mats = owner_ref.shape[1]
    devices = table_ref.shape[1]
    f32 = jnp.float32

    def iota(rows, cols, axis):
        return lax.broadcasted_iota(jnp.int32, (rows, cols), axis)

    def total(cond, axis):
        return jnp.sum(jnp.where(cond, 1.0, 0.0).astype(f32), axis=axis, keepdims=True)

    def column(row):
        n = row.shape[1]
        return jnp.sum(jnp.where(iota(n, n, 0) == iota(n, n, 1), row, 0.0), axis=1, keepdims=True)

    own_row = owner_ref[...].astype(f32)
    own_col = column(own_row)
    same = own_col == own_row
    rank_row = total(same & (iota(mats, mats, 0) < iota(mats, mats, 1)), 0)
    rank_col = total(same & (iota(mats, mats, 1) < iota(mats, mats, 0)), 1)
    held = own_col == iota(mats, devices, 1).astype(f32)
    first_row = total(held & (rank_col == 0.0), 0)
    second_row = total(held & (rank_col == 1.0), 0)
    held = own_row == iota(devices, mats, 0).astype(f32)
    first_col = total(held & (rank_row == 0.0), 1)
    second_col = total(held & (rank_row == 1.0), 1)
    up, down = iota(devices, devices, 0), iota(devices, devices, 1)
    plane = (up & (planes - 1)) == (down & (planes - 1))
    before_row, before_col = up < down, down < up
    free_index = total(before_col & plane & (first_row == 0.0), 1)
    second_index = total(before_row & plane & (second_col == 1.0), 0)
    pair = plane & (first_col == 0.0) & (second_row == 1.0) & (free_index == second_index)
    left_row = second_row - total(pair, 0)
    idle_col = 1.0 - first_col - total(pair, 1)
    left_col = column(left_row)
    idle_row = jnp.sum(jnp.where(up == down, idle_col, 0.0), axis=0, keepdims=True)
    left_index = total(before_row & (left_col == 1.0), 0)
    idle_index = total(before_col & (idle_row == 1.0), 1)
    spill = (left_row == 1.0) & (idle_col == 1.0) & (left_index == idle_index)
    helper_row = jnp.sum(jnp.where(pair | spill, up.astype(f32), 0.0), axis=0, keepdims=True)
    helper_col = column(helper_row)
    helper_of = jnp.sum(jnp.where(held, helper_col, 0.0), axis=0, keepdims=True)
    slot_row = jnp.where(rank_row == 0.0, own_row, helper_of)
    spilled = jnp.sum(left_row, axis=1, keepdims=True)
    table_ref[...] = jnp.zeros_like(table_ref)
    table_ref[SLOT : SLOT + 1, :mats] = slot_row.astype(jnp.int32)
    table_ref[HELPER : HELPER + 1, :] = helper_row.astype(jnp.int32)
    table_ref[FIRST : FIRST + 1, :] = first_row.astype(jnp.int32)
    table_ref[SECOND : SECOND + 1, :] = second_row.astype(jnp.int32)
    table_ref[SPILLED : SPILLED + 1, :] = jnp.broadcast_to(spilled, (1, devices)).astype(jnp.int32)


def make_table(owner_table, planes, devices):
    mats = owner_table.shape[0]
    return pl.pallas_call(
        functools.partial(table_kernel, planes),
        out_shape=jax.ShapeDtypeStruct((TABLE_ROWS, devices), jnp.int32),
        name="table",
    )(owner_table.reshape(1, mats))


def momentum_kernel(table_ref, momentum_ref, grad_ref, new_ref, out_ref):
    step = pl.program_id(0)
    block = momentum_ref.shape[0]

    @pl.when(step == 0)
    def _():
        out_ref[...] = jnp.zeros_like(out_ref)

    for i in range(block):
        grad = grad_ref[i].astype(jnp.float32)
        new = momentum_decay * momentum_ref[i] + grad
        new_ref[i] = new
        slot = table_ref[SLOT, step * block + i]
        out_ref[slot] = (grad + momentum_decay * new).astype(out_ref.dtype)


def momentum_step(table, momentum, grad, devices, block=24):
    mats, rows, cols = momentum.shape
    while mats % block:
        block -= 1

    def block_spec():
        return pl.BlockSpec((block, rows, cols), lambda i, *_: (i, 0, 0))

    return pl.pallas_call(
        momentum_kernel,
        grid_spec=pltpu.PrefetchScalarGridSpec(
            num_scalar_prefetch=1,
            grid=(mats // block,),
            in_specs=[block_spec(), block_spec()],
            out_specs=[block_spec(), pl.BlockSpec((devices, rows, cols), lambda i, *_: (0, 0, 0))],
        ),
        out_shape=[
            jax.ShapeDtypeStruct(momentum.shape, jnp.float32),
            jax.ShapeDtypeStruct((devices, rows, cols), jnp.bfloat16),
        ],
        compiler_params=pltpu.CompilerParams(vmem_limit_bytes=32 * 1024 * 1024),
        name="momentum",
    )(table, momentum, grad)


def orthogonalize_kernel(scale, x_ref, out_ref, iterate_ref, gram_ref, poly_ref):
    rows, cols = x_ref.shape
    tile = min(256, rows)
    f32, bf16 = jnp.float32, jnp.bfloat16

    def poly(gram):
        gram_ref[...] = gram.astype(bf16)
        square = jnp.dot(gram_ref[...], gram_ref[...], preferred_element_type=f32)
        poly_ref[...] = (quintic_two * gram_ref[...].astype(f32) + quintic_three * square).astype(bf16)

    def apply(source_ref, target_ref, factor, last):
        for i in range(rows // tile):
            part = source_ref[i * tile : (i + 1) * tile, :]
            step = quintic_one * part.astype(f32) + jnp.dot(part, poly_ref[...], preferred_element_type=f32)
            step = (step * factor).astype(bf16) if factor is not None else step.astype(bf16)
            target_ref[i * tile : (i + 1) * tile, :] = step * jnp.asarray(scale, bf16) if last else step

    def gram_of(ref):
        return lax.dot_general(ref[...], ref[...], (((0,), (0,)), ((), ())), preferred_element_type=f32)

    gram = gram_of(x_ref)
    diagonal = lax.broadcasted_iota(jnp.int32, (cols, cols), 0) == lax.broadcasted_iota(jnp.int32, (cols, cols), 1)
    trace = jnp.sum(jnp.sum(jnp.where(diagonal, gram, 0.0), axis=0, keepdims=True), axis=1, keepdims=True)
    factor = 1.0 / (jnp.sqrt(trace) + norm_epsilon)
    poly(gram * factor * factor)
    apply(x_ref, iterate_ref, factor, False)
    for step in range(1, ITERS):
        poly(gram_of(iterate_ref))
        apply(iterate_ref, out_ref, None, True)


def orthogonalize(matrix, scale):
    rows, cols = matrix.shape
    return pl.pallas_call(
        functools.partial(orthogonalize_kernel, scale),
        out_shape=jax.ShapeDtypeStruct((rows, cols), jnp.bfloat16),
        scratch_shapes=[
            pltpu.VMEM((rows, cols), jnp.bfloat16),
            pltpu.VMEM((cols, cols), jnp.bfloat16),
            pltpu.VMEM((cols, cols), jnp.bfloat16),
        ],
        compiler_params=pltpu.CompilerParams(vmem_limit_bytes=40 * 1024 * 1024),
        cost_estimate=pl.CostEstimate(flops=ITERS * 2 * cols * cols * (2 * rows + cols), bytes_accessed=4 * rows * cols, transcendentals=0),
        name="orthogonalize",
    )(matrix)


def pick_kernel(planes, table_ref, place_ref, parts_ref, out_ref, sem):
    def each(i):
        helper = table_ref[HELPER, i * planes + place_ref[0]]
        return pltpu.make_async_copy(parts_ref.at[lax.div(helper, planes)], out_ref.at[i], sem.at[i])

    count = out_ref.shape[0]
    lax.fori_loop(0, count, lambda i, _: each(i).start(), None)
    lax.fori_loop(0, count, lambda i, _: each(i).wait(), None)


def pick(table, place, parts, planes):
    return pl.pallas_call(
        functools.partial(pick_kernel, planes),
        grid_spec=pltpu.PrefetchScalarGridSpec(
            num_scalar_prefetch=2,
            grid=(),
            in_specs=[pl.BlockSpec(memory_space=pl.ANY)],
            out_specs=pl.BlockSpec(memory_space=pl.ANY),
            scratch_shapes=[pltpu.SemaphoreType.DMA((parts.shape[0],))],
        ),
        out_shape=jax.ShapeDtypeStruct(parts.shape, parts.dtype),
        name="pick",
    )(table, place, parts)


def row_index(place_ref, planes, count, slot):
    far = lax.rem(place_ref[0] - lax.rem(slot, planes) + planes, planes)
    return far * count + lax.div(slot, planes)


def update_kernel(planes, table_ref, place_ref, rows_ref, update_ref):
    step = pl.program_id(0)
    block = update_ref.shape[0]
    count = rows_ref.shape[0] // planes
    for i in range(block):
        slot = table_ref[SLOT, step * block + i]
        update_ref[i] = rows_ref[row_index(place_ref, planes, count, slot)].astype(jnp.float32)


def spread_update(table, place, arrived, mats, planes, block=24):
    slots, rows, cols = arrived.shape
    while mats % block:
        block -= 1
    return pl.pallas_call(
        functools.partial(update_kernel, planes),
        grid_spec=pltpu.PrefetchScalarGridSpec(
            num_scalar_prefetch=2,
            grid=(mats // block,),
            in_specs=[pl.BlockSpec((slots, rows, cols), lambda i, *_: (0, 0, 0))],
            out_specs=pl.BlockSpec((block, rows, cols), lambda i, *_: (i, 0, 0)),
        ),
        out_shape=jax.ShapeDtypeStruct((mats, rows, cols), jnp.float32),
        compiler_params=pltpu.CompilerParams(vmem_limit_bytes=32 * 1024 * 1024),
        name="update",
    )(table, place, arrived)


def spilled_kernel(planes, table_ref, place_ref, rows_ref, out_ref):
    count = rows_ref.shape[0] // planes

    def each(i, _):
        out_ref[i] = rows_ref[row_index(place_ref, planes, count, table_ref[HELPER, i])]

    lax.fori_loop(0, out_ref.shape[0], each, None)


def spilled_rows(table, place, arrived, planes):
    whole = pl.BlockSpec(arrived.shape, lambda *_: (0, 0, 0))
    return pl.pallas_call(
        functools.partial(spilled_kernel, planes),
        grid_spec=pltpu.PrefetchScalarGridSpec(num_scalar_prefetch=2, grid=(1,), in_specs=[whole], out_specs=whole),
        out_shape=jax.ShapeDtypeStruct(arrived.shape, arrived.dtype),
        compiler_params=pltpu.CompilerParams(vmem_limit_bytes=32 * 1024 * 1024),
        name="spilled",
    )(table, place, arrived)


def owned_kernel(table_ref, place_ref, first_ref, second_ref, out_ref, zero_ref, sem):
    rows = out_ref.shape[1]
    tile = zero_ref.shape[0]
    zero_ref[...] = jnp.zeros_like(zero_ref)
    me = place_ref[1]

    def slot(index, source_ref, act):
        present = table_ref[FIRST + index, me] > 0

        @pl.when(present)
        def _():
            act(pltpu.make_async_copy(source_ref, out_ref.at[index], sem.at[index, 0]))

        @pl.when(jnp.logical_not(present))
        def _():
            for i in range(rows // tile):
                act(pltpu.make_async_copy(zero_ref, out_ref.at[index, pl.ds(i * tile, tile)], sem.at[index, i]))

    for act in (lambda copy: copy.start(), lambda copy: copy.wait()):
        slot(0, first_ref, act)
        slot(1, second_ref, act)


def place_owned(table, place, first, second):
    rows, cols = first.shape
    tile = min(256, rows)
    hbm = pl.BlockSpec(memory_space=pl.ANY)
    return pl.pallas_call(
        owned_kernel,
        grid_spec=pltpu.PrefetchScalarGridSpec(
            num_scalar_prefetch=2,
            grid=(),
            in_specs=[hbm, hbm],
            out_specs=hbm,
            scratch_shapes=[
                pltpu.VMEM((tile, cols), first.dtype),
                pltpu.SemaphoreType.DMA((CAP, rows // tile)),
            ],
        ),
        out_shape=jax.ShapeDtypeStruct((CAP, rows, cols), first.dtype),
        name="owned",
    )(table, place, first, second)


def shards(momentum, grad, owner_table):
    dp_count = lax.axis_size("dp")
    planes = lax.axis_size("owner")
    devices = dp_count * planes
    mats, rows, cols = momentum.shape
    whole_rows = devices * rows
    my_plane = lax.axis_index("owner")
    place = jnp.stack([my_plane, lax.axis_index("dp") * planes + my_plane]).astype(jnp.int32)
    with jax.named_scope("table"):
        table = make_table(owner_table, planes, devices)
    with jax.named_scope("momentum"):
        new_momentum, outgoing = momentum_step(table, momentum, grad, devices)
    with jax.named_scope("gather_matrix"):
        received = lax.all_to_all(outgoing, ("dp", "owner"), 0, 0, tiled=True)
        matrix = received.reshape(whole_rows, cols)
    with jax.named_scope("orthogonalize"):
        mine = orthogonalize(matrix, math.sqrt(whole_rows))
    with jax.named_scope("return_dp"):
        parts = lax.all_to_all(mine.reshape(dp_count, planes * rows, cols), "dp", 0, 0, tiled=True)
    with jax.named_scope("return_owner"):
        by_plane = parts.reshape(dp_count, planes, rows, cols)

        def to_plane(far):
            return lax.dynamic_index_in_dim(by_plane, lax.rem(my_plane + far, planes), 1, keepdims=False)

        arrived = {0: to_plane(0)}
        for far in sorted(range(1, planes), key=lambda far: -min(far, planes - far)):
            arrived[far] = lax.ppermute(to_plane(far), "owner", [(i, (i + far) % planes) for i in range(planes)])
        arrived = jnp.concatenate([arrived[far] for far in range(planes)])
    with jax.named_scope("second_matrix"):
        second = lax.all_to_all(pick(table, place, parts, planes), "dp", 0, 0, tiled=True).reshape(whole_rows, cols)
    with jax.named_scope("owned"):
        owned = place_owned(table, place, mine, second)
    with jax.named_scope("update"):
        update = spread_update(table, place, arrived, mats, planes)

    def with_spilled(owned, arrived):
        rows_out = lax.all_to_all(spilled_rows(table, place, arrived, planes), ("dp", "owner"), 0, 0, tiled=True)
        return place_owned(table, place, mine, rows_out.reshape(whole_rows, cols))

    with jax.named_scope("spilled"):
        owned = lax.cond(table[SPILLED, 0] > 0, with_spilled, lambda owned, arrived: owned, owned, arrived)
    return new_momentum, update, owned[:, None]


def solution(mesh):
    in_specs = (P(None, ("dp", "owner"), None), P(None, ("dp", "owner"), None), P())
    out_specs = (
        P(None, ("dp", "owner"), None),
        P(None, ("dp", "owner"), None),
        P(None, ("dp", "owner"), None, None),
    )
    return jax.shard_map(shards, mesh=mesh, in_specs=in_specs, out_specs=out_specs, check_vma=False)
```

```python
import functools
import math

import jax
import jax.numpy as jnp
from jax import lax
from jax.experimental import pallas as pl
from jax.experimental.pallas import tpu as pltpu
from jax.sharding import PartitionSpec as P

ITERS = 2
CAP = 2

momentum_decay = 0.95
quintic_one = 3.4445
quintic_two = -4.775
quintic_three = 2.0315
norm_epsilon = 1e-07

SLOT, FIRST, SECOND, SPILLED, PART, INDEX, EARLY, HELPER_INDEX, HELPER_EARLY = range(9)
TABLE_ROWS = 16


def table_kernel(planes, place_ref, owner_ref, table_ref):
    mats = owner_ref.shape[1]
    devices = table_ref.shape[1]
    f32 = jnp.float32

    def iota(rows, cols, axis):
        return lax.broadcasted_iota(jnp.int32, (rows, cols), axis)

    def total(cond, axis):
        return jnp.sum(jnp.where(cond, 1.0, 0.0).astype(f32), axis=axis, keepdims=True)

    def column(row):
        n = row.shape[1]
        return jnp.sum(jnp.where(iota(n, n, 0) == iota(n, n, 1), row, 0.0), axis=1, keepdims=True)

    own_row = owner_ref[...].astype(f32)
    own_col = column(own_row)
    same = own_col == own_row
    rank_row = total(same & (iota(mats, mats, 0) < iota(mats, mats, 1)), 0)
    rank_col = total(same & (iota(mats, mats, 1) < iota(mats, mats, 0)), 1)
    held = own_col == iota(mats, devices, 1).astype(f32)
    first_row = total(held & (rank_col == 0.0), 0)
    second_row = total(held & (rank_col == 1.0), 0)
    held = own_row == iota(devices, mats, 0).astype(f32)
    first_col = total(held & (rank_row == 0.0), 1)
    second_col = total(held & (rank_row == 1.0), 1)
    up, down = iota(devices, devices, 0), iota(devices, devices, 1)
    plane = (up & (planes - 1)) == (down & (planes - 1))
    before_row, before_col = up < down, down < up
    free_index = total(before_col & plane & (first_row == 0.0), 1)
    second_index = total(before_row & plane & (second_col == 1.0), 0)
    pair = plane & (first_col == 0.0) & (second_row == 1.0) & (free_index == second_index)
    left_row = second_row - total(pair, 0)
    idle_col = 1.0 - first_col - total(pair, 1)
    left_col = column(left_row)
    idle_row = jnp.sum(jnp.where(up == down, idle_col, 0.0), axis=0, keepdims=True)
    left_index = total(before_row & (left_col == 1.0), 0)
    idle_index = total(before_col & (idle_row == 1.0), 1)
    spill = (left_row == 1.0) & (idle_col == 1.0) & (left_index == idle_index)
    helper_row = jnp.sum(jnp.where(pair | spill, up.astype(f32), 0.0), axis=0, keepdims=True)
    helper_col = column(helper_row)
    helper_of = jnp.sum(jnp.where(held, helper_col, 0.0), axis=0, keepdims=True)
    slot_row = jnp.where(rank_row == 0.0, own_row, helper_of)
    spilled = jnp.sum(left_row, axis=1, keepdims=True)
    slot_row = slot_row.astype(jnp.int32)
    helper_row = helper_row.astype(jnp.int32)
    shift = planes.bit_length() - 1
    count = devices // planes

    def late_index(slot):
        return ((place_ref[0] - slot) & (planes - 1)) * count + (slot >> shift)

    def early_index(slot):
        return (slot >> shift) * planes + ((place_ref[0] - slot) & (planes - 1))

    mine = up == (down * planes + place_ref[0])
    helper_here = column(helper_row.astype(f32))
    part_row = jnp.sum(jnp.where(mine, helper_here, 0.0), axis=0, keepdims=True).astype(jnp.int32) >> shift

    def put(row, values):
        table_ref[row : row + 1, : values.shape[1]] = values.astype(jnp.int32)

    table_ref[...] = jnp.zeros_like(table_ref)
    put(SLOT, slot_row)
    put(FIRST, first_row)
    put(SECOND, second_row)
    put(SPILLED, jnp.broadcast_to(spilled, (1, devices)))
    put(PART, part_row)
    put(INDEX, late_index(slot_row))
    put(EARLY, early_index(slot_row))
    put(HELPER_INDEX, late_index(helper_row))
    put(HELPER_EARLY, early_index(helper_row))


def make_table(owner_table, place, planes, devices):
    mats = owner_table.shape[0]
    return pl.pallas_call(
        functools.partial(table_kernel, planes),
        grid_spec=pltpu.PrefetchScalarGridSpec(
            num_scalar_prefetch=1,
            grid=(1,),
            in_specs=[pl.BlockSpec((1, mats), lambda *_: (0, 0))],
            out_specs=pl.BlockSpec((TABLE_ROWS, devices), lambda *_: (0, 0)),
        ),
        out_shape=jax.ShapeDtypeStruct((TABLE_ROWS, devices), jnp.int32),
        name="table",
    )(place, owner_table.reshape(1, mats))


def momentum_kernel(table_ref, momentum_ref, grad_ref, new_ref, out_ref):
    step = pl.program_id(0)
    block = momentum_ref.shape[0]

    @pl.when(step == 0)
    def _():
        out_ref[...] = jnp.zeros_like(out_ref)

    for i in range(block):
        grad = grad_ref[i].astype(jnp.float32)
        new = momentum_decay * momentum_ref[i] + grad
        new_ref[i] = new
        slot = table_ref[SLOT, step * block + i]
        out_ref[slot] = (grad + momentum_decay * new).astype(out_ref.dtype)


def momentum_step(table, momentum, grad, devices, block=24):
    mats, rows, cols = momentum.shape
    while mats % block:
        block -= 1

    def block_spec():
        return pl.BlockSpec((block, rows, cols), lambda i, *_: (i, 0, 0))

    return pl.pallas_call(
        momentum_kernel,
        grid_spec=pltpu.PrefetchScalarGridSpec(
            num_scalar_prefetch=1,
            grid=(mats // block,),
            in_specs=[block_spec(), block_spec()],
            out_specs=[block_spec(), pl.BlockSpec((devices, rows, cols), lambda i, *_: (0, 0, 0))],
        ),
        out_shape=[
            jax.ShapeDtypeStruct(momentum.shape, jnp.float32),
            jax.ShapeDtypeStruct((devices, rows, cols), jnp.bfloat16),
        ],
        compiler_params=pltpu.CompilerParams(vmem_limit_bytes=60 * 1024 * 1024),
        name="momentum",
    )(table, momentum, grad)


def orthogonalize_kernel(scale, x_ref, out_ref, iterate_ref, gram_ref, poly_ref):
    rows, cols = x_ref.shape
    tile = min(256, rows)
    f32, bf16 = jnp.float32, jnp.bfloat16

    def poly(gram):
        gram_ref[...] = gram.astype(bf16)
        square = jnp.dot(gram_ref[...], gram_ref[...], preferred_element_type=f32)
        poly_ref[...] = (quintic_two * gram_ref[...].astype(f32) + quintic_three * square).astype(bf16)

    def apply(source_ref, target_ref, factor, last):
        for i in range(rows // tile):
            part = source_ref[i * tile : (i + 1) * tile, :]
            step = quintic_one * part.astype(f32) + jnp.dot(part, poly_ref[...], preferred_element_type=f32)
            step = (step * factor).astype(bf16) if factor is not None else step.astype(bf16)
            target_ref[i * tile : (i + 1) * tile, :] = step * jnp.asarray(scale, bf16) if last else step

    def gram_of(ref):
        return lax.dot_general(ref[...], ref[...], (((0,), (0,)), ((), ())), preferred_element_type=f32)

    gram = gram_of(x_ref)
    diagonal = lax.broadcasted_iota(jnp.int32, (cols, cols), 0) == lax.broadcasted_iota(jnp.int32, (cols, cols), 1)
    trace = jnp.sum(jnp.sum(jnp.where(diagonal, gram, 0.0), axis=0, keepdims=True), axis=1, keepdims=True)
    factor = 1.0 / (jnp.sqrt(trace) + norm_epsilon)
    poly(gram * factor * factor)
    apply(x_ref, iterate_ref, factor, False)
    for step in range(1, ITERS):
        poly(gram_of(iterate_ref))
        apply(iterate_ref, out_ref, None, True)


def orthogonalize(matrix, scale):
    rows, cols = matrix.shape
    return pl.pallas_call(
        functools.partial(orthogonalize_kernel, scale),
        out_shape=jax.ShapeDtypeStruct((rows, cols), jnp.bfloat16),
        scratch_shapes=[
            pltpu.VMEM((rows, cols), jnp.bfloat16),
            pltpu.VMEM((cols, cols), jnp.bfloat16),
            pltpu.VMEM((cols, cols), jnp.bfloat16),
        ],
        compiler_params=pltpu.CompilerParams(vmem_limit_bytes=40 * 1024 * 1024),
        cost_estimate=pl.CostEstimate(flops=ITERS * 2 * cols * cols * (2 * rows + cols), bytes_accessed=4 * rows * cols, transcendentals=0),
        name="orthogonalize",
    )(matrix)


def pack_kernel(table_ref, place_ref, parts_ref, early_ref, out_ref):
    count, _, cols = parts_ref.shape
    out_ref[:, :, cols:] = early_ref[...]

    def each(i, _):
        out_ref[i, :, :cols] = parts_ref[table_ref[PART, i]]

    lax.fori_loop(0, count, each, None, unroll=True)


def pack(table, place, parts, early):
    count, rows, cols = parts.shape
    shape = (count, rows, cols + early.shape[2])
    return pl.pallas_call(
        pack_kernel,
        grid_spec=pltpu.PrefetchScalarGridSpec(
            num_scalar_prefetch=2,
            grid=(1,),
            in_specs=[pl.BlockSpec(x.shape, lambda *_: (0, 0, 0)) for x in (parts, early)],
            out_specs=pl.BlockSpec(shape, lambda *_: (0, 0, 0)),
        ),
        out_shape=jax.ShapeDtypeStruct(shape, parts.dtype),
        compiler_params=pltpu.CompilerParams(vmem_limit_bytes=24 * 1024 * 1024),
        name="pack",
    )(table, place, parts, early)


def finish_kernel(table_ref, place_ref, late_ref, early_ref, mine_ref, second_ref, update_ref, owned_ref):
    step = pl.program_id(0)
    block = update_ref.shape[0]
    late_cols = late_ref.shape[2]
    for i in range(block):
        index = table_ref[INDEX, step * block + i]
        update_ref[i, :, :late_cols] = late_ref[index].astype(jnp.float32)
        index = table_ref[EARLY, step * block + i]
        update_ref[i, :, late_cols:] = early_ref[index].astype(jnp.float32)
    me = place_ref[1]
    write_owned(table_ref, me, mine_ref[...], second_ref, owned_ref)


def write_owned(table_ref, me, mine, second_ref, owned_ref):
    cols = mine.shape[1]
    second = second_ref[...].reshape(mine.shape[0], second_ref.shape[2])[:, :cols]
    owned_ref[0] = jnp.where(table_ref[FIRST, me] > 0, mine, jnp.zeros_like(mine))
    owned_ref[1] = jnp.where(table_ref[SECOND, me] > 0, second, jnp.zeros_like(second))


def finish(table, place, late, early, mine, second, mats, steps=8):
    while mats % steps or second.shape[0] % steps:
        steps -= 1
    _, rows, _ = late.shape
    whole_rows, cols = mine.shape
    second_block = (second.shape[0] // steps, *second.shape[1:])
    return pl.pallas_call(
        finish_kernel,
        grid_spec=pltpu.PrefetchScalarGridSpec(
            num_scalar_prefetch=2,
            grid=(steps,),
            in_specs=[
                pl.BlockSpec(late.shape, lambda i, *_: (0, 0, 0)),
                pl.BlockSpec(early.shape, lambda i, *_: (0, 0, 0)),
                pl.BlockSpec((whole_rows // steps, cols), lambda i, *_: (i, 0)),
                pl.BlockSpec(second_block, lambda i, *_: (i, 0, 0)),
            ],
            out_specs=[
                pl.BlockSpec((mats // steps, rows, cols), lambda i, *_: (i, 0, 0)),
                pl.BlockSpec((CAP, whole_rows // steps, cols), lambda i, *_: (0, i, 0)),
            ],
        ),
        out_shape=[
            jax.ShapeDtypeStruct((mats, rows, cols), jnp.float32),
            jax.ShapeDtypeStruct((CAP, whole_rows, cols), mine.dtype),
        ],
        compiler_params=pltpu.CompilerParams(vmem_limit_bytes=32 * 1024 * 1024),
        name="finish",
    )(table, place, late, early, mine, second)


def spilled_kernel(table_ref, place_ref, late_ref, early_ref, out_ref):
    late_cols = late_ref.shape[2]

    def each(i, _):
        out_ref[i, :, :late_cols] = late_ref[table_ref[HELPER_INDEX, i]]
        out_ref[i, :, late_cols:] = early_ref[table_ref[HELPER_EARLY, i]]

    lax.fori_loop(0, out_ref.shape[0], each, None)


def spilled_rows(table, place, late, early):
    shape = (late.shape[0], late.shape[1], late.shape[2] + early.shape[2])
    return pl.pallas_call(
        spilled_kernel,
        grid_spec=pltpu.PrefetchScalarGridSpec(
            num_scalar_prefetch=2,
            grid=(1,),
            in_specs=[pl.BlockSpec(x.shape, lambda *_: (0, 0, 0)) for x in (late, early)],
            out_specs=pl.BlockSpec(shape, lambda *_: (0, 0, 0)),
        ),
        out_shape=jax.ShapeDtypeStruct(shape, late.dtype),
        compiler_params=pltpu.CompilerParams(vmem_limit_bytes=32 * 1024 * 1024),
        name="spilled",
    )(table, place, late, early)


def replace_kernel(table_ref, place_ref, mine_ref, second_ref, owned_ref):
    write_owned(table_ref, place_ref[1], mine_ref[...], second_ref, owned_ref)


def replace_owned(table, place, mine, second):
    shape = (CAP, *mine.shape)
    return pl.pallas_call(
        replace_kernel,
        grid_spec=pltpu.PrefetchScalarGridSpec(
            num_scalar_prefetch=2,
            grid=(1,),
            in_specs=[
                pl.BlockSpec(mine.shape, lambda *_: (0, 0)),
                pl.BlockSpec(second.shape, lambda *_: (0, 0, 0)),
            ],
            out_specs=pl.BlockSpec(shape, lambda *_: (0, 0, 0)),
        ),
        out_shape=jax.ShapeDtypeStruct(shape, mine.dtype),
        compiler_params=pltpu.CompilerParams(vmem_limit_bytes=32 * 1024 * 1024),
        name="replace",
    )(table, place, mine, second)


def send_planes(rows, axis):
    planes = lax.axis_size("owner")
    me = lax.axis_index("owner")

    def to_plane(far):
        return lax.dynamic_index_in_dim(rows, lax.rem(me + far, planes), axis, keepdims=False)

    arrived = {0: to_plane(0)}
    for far in sorted(range(1, planes), key=lambda far: -min(far, planes - far)):
        arrived[far] = lax.ppermute(to_plane(far), "owner", [(i, (i + far) % planes) for i in range(planes)])
    return [arrived[far] for far in range(planes)]


def shards(momentum, grad, owner_table):
    dp_count = lax.axis_size("dp")
    planes = lax.axis_size("owner")
    devices = dp_count * planes
    mats, rows, cols = momentum.shape
    whole_rows = devices * rows
    late_cols = cols - cols // 3 if cols % 384 == 0 else cols - 128
    my_plane = lax.axis_index("owner")
    place = jnp.stack([my_plane, lax.axis_index("dp") * planes + my_plane]).astype(jnp.int32)
    with jax.named_scope("table"):
        table = make_table(owner_table, place, planes, devices)
    with jax.named_scope("momentum"):
        new_momentum, outgoing = momentum_step(table, momentum, grad, devices)
    with jax.named_scope("gather_matrix"):
        received = lax.all_to_all(outgoing, ("dp", "owner"), 0, 0, tiled=True)
        matrix = received.reshape(whole_rows, cols)
    with jax.named_scope("orthogonalize"):
        mine = orthogonalize(matrix, math.sqrt(whole_rows))
    with jax.named_scope("return_dp"):
        parts = lax.all_to_all(mine.reshape(dp_count, planes * rows, cols), "dp", 0, 0, tiled=True)
    with jax.named_scope("return_owner_early"):
        early = send_planes(mine.reshape(dp_count, planes, rows, cols)[..., late_cols:], 1)
        early = jnp.stack(early, 1).reshape(dp_count, planes * rows, cols - late_cols)
    with jax.named_scope("return_owner"):
        late = jnp.concatenate(send_planes(parts.reshape(dp_count, planes, rows, cols)[..., :late_cols], 1))
    with jax.named_scope("second_matrix"):
        second = lax.all_to_all(pack(table, place, parts, early), "dp", 0, 0, tiled=True)
        early = second[..., cols:].reshape(devices, rows, cols - late_cols)
    with jax.named_scope("finish"):
        update, owned = finish(table, place, late, early, mine, second, mats)

    def with_spilled(owned, late, early):
        rows_out = lax.all_to_all(spilled_rows(table, place, late, early), ("dp", "owner"), 0, 0, tiled=True)
        return replace_owned(table, place, mine, rows_out.reshape(dp_count, planes * rows, cols))

    with jax.named_scope("spilled"):
        spilled = table[SPILLED, 0] > 0
        owned = lax.cond(spilled, with_spilled, lambda owned, late, early: owned, owned, late, early)
    return new_momentum, update, owned[:, None]


def solution(mesh):
    in_specs = (P(None, ("dp", "owner"), None), P(None, ("dp", "owner"), None), P())
    out_specs = (
        P(None, ("dp", "owner"), None),
        P(None, ("dp", "owner"), None),
        P(None, ("dp", "owner"), None, None),
    )
    return jax.shard_map(shards, mesh=mesh, in_specs=in_specs, out_specs=out_specs, check_vma=False)
```

```python
import functools
import math

import jax
import jax.numpy as jnp
from jax import lax
from jax.experimental import pallas as pl
from jax.experimental.pallas import tpu as pltpu
from jax.sharding import PartitionSpec as P

ITERS = 2
CAP = 2

momentum_decay = 0.95
quintic_one = 3.4445
quintic_two = -4.775
quintic_three = 2.0315
norm_epsilon = 1e-07

SLOT, FIRST, SECOND, SPILLED, PART, MATRIX, HELPER_INDEX = range(7)
TABLE_ROWS = 8


def early_distances(planes):
    return [planes // 2 - 1, planes // 2 + 1]


def late_distances(planes):
    early = early_distances(planes)
    return sorted((far for far in range(1, planes) if far not in early), key=lambda far: -min(far, planes - far))


def distances(planes):
    return [0, *late_distances(planes), *early_distances(planes)]


def fill_table(planes, place_ref, owner_ref, table_ref):
    mats = owner_ref.shape[1]
    devices = table_ref.shape[1]
    f32 = jnp.float32

    def iota(rows, cols, axis):
        return lax.broadcasted_iota(jnp.int32, (rows, cols), axis)

    def total(cond, axis):
        return jnp.sum(jnp.where(cond, 1.0, 0.0).astype(f32), axis=axis, keepdims=True)

    def column(row):
        n = row.shape[1]
        return jnp.sum(jnp.where(iota(n, n, 0) == iota(n, n, 1), row, 0.0), axis=1, keepdims=True)

    own_row = owner_ref[...].astype(f32)
    own_col = column(own_row)
    same = own_col == own_row
    rank_row = total(same & (iota(mats, mats, 0) < iota(mats, mats, 1)), 0)
    rank_col = total(same & (iota(mats, mats, 1) < iota(mats, mats, 0)), 1)
    held = own_col == iota(mats, devices, 1).astype(f32)
    first_row = total(held & (rank_col == 0.0), 0)
    second_row = total(held & (rank_col == 1.0), 0)
    held = own_row == iota(devices, mats, 0).astype(f32)
    first_col = total(held & (rank_row == 0.0), 1)
    second_col = total(held & (rank_row == 1.0), 1)
    up, down = iota(devices, devices, 0), iota(devices, devices, 1)
    plane = (up & (planes - 1)) == (down & (planes - 1))
    before_row, before_col = up < down, down < up
    free_index = total(before_col & plane & (first_row == 0.0), 1)
    second_index = total(before_row & plane & (second_col == 1.0), 0)
    pair = plane & (first_col == 0.0) & (second_row == 1.0) & (free_index == second_index)
    left_row = second_row - total(pair, 0)
    idle_col = 1.0 - first_col - total(pair, 1)
    left_col = column(left_row)
    idle_row = jnp.sum(jnp.where(up == down, idle_col, 0.0), axis=0, keepdims=True)
    left_index = total(before_row & (left_col == 1.0), 0)
    idle_index = total(before_col & (idle_row == 1.0), 1)
    spill = (left_row == 1.0) & (idle_col == 1.0) & (left_index == idle_index)
    helper_row = jnp.sum(jnp.where(pair | spill, up.astype(f32), 0.0), axis=0, keepdims=True)
    helper_col = column(helper_row)
    helper_of = jnp.sum(jnp.where(held, helper_col, 0.0), axis=0, keepdims=True)
    slot_row = jnp.where(rank_row == 0.0, own_row, helper_of)
    spilled = jnp.sum(left_row, axis=1, keepdims=True)
    slot_row = slot_row.astype(jnp.int32)
    helper_row = helper_row.astype(jnp.int32)
    shift = planes.bit_length() - 1
    count = devices // planes

    order = distances(planes)

    def arrival(slot):
        far = (place_ref[0] - slot) & (planes - 1)
        position = sum(jnp.where(far == distance, i, 0) for i, distance in enumerate(order))
        return position * count + (slot >> shift)

    slot_col = column(slot_row.astype(f32)).astype(jnp.int32)
    lands = arrival(slot_col) == iota(mats, devices, 1)
    matrix_row = jnp.sum(jnp.where(lands, iota(mats, devices, 0) + 1, 0).astype(f32), axis=0, keepdims=True) - 1.0

    mine = up == (down * planes + place_ref[0])
    helper_here = column(helper_row.astype(f32))
    part_row = jnp.sum(jnp.where(mine, helper_here, 0.0), axis=0, keepdims=True).astype(jnp.int32) >> shift

    def put(row, values):
        table_ref[row : row + 1, : values.shape[1]] = values.astype(jnp.int32)

    table_ref[...] = jnp.zeros_like(table_ref)
    put(SLOT, slot_row)
    put(FIRST, first_row)
    put(SECOND, second_row)
    put(SPILLED, jnp.broadcast_to(spilled, (1, devices)))
    put(PART, part_row)
    put(MATRIX, matrix_row)
    put(HELPER_INDEX, arrival(helper_row))


def start_kernel(
    planes, place_ref, owner_ref, momentum_ref, grad_ref, table_ref, new_ref, out_ref, new, grad, slots, in_sem, out_sem, slot_sem
):
    chunks = in_sem.shape[1]
    block = new.shape[0] // chunks

    def part(chunk):
        return pl.ds(chunk * block, block)

    def copies_in(chunk):
        return (
            pltpu.make_async_copy(momentum_ref.at[part(chunk)], new.at[part(chunk)], in_sem.at[0, chunk]),
            pltpu.make_async_copy(grad_ref.at[part(chunk)], grad.at[part(chunk)], in_sem.at[1, chunk]),
        )

    def copy_out(chunk):
        return pltpu.make_async_copy(new.at[part(chunk)], new_ref.at[part(chunk)], out_sem.at[chunk])

    for chunk in range(chunks):
        for copy in copies_in(chunk):
            copy.start()
    fill_table(planes, place_ref, owner_ref, table_ref)
    slot_copy = pltpu.make_async_copy(table_ref.at[pl.ds(0, 8)], slots, slot_sem)
    slot_copy.start()
    out_ref[...] = jnp.zeros_like(out_ref)
    slot_copy.wait()

    def each(chunk, _):
        for copy in copies_in(chunk):
            copy.wait()
        for i in range(block):
            mat = chunk * block + i
            value = grad[mat].astype(jnp.float32)
            result = momentum_decay * new[mat] + value
            new[mat] = result
            out_ref[slots[SLOT, mat]] = (value + momentum_decay * result).astype(out_ref.dtype)
        copy_out(chunk).start()

    lax.fori_loop(0, chunks, each, None)
    for chunk in range(chunks):
        copy_out(chunk).wait()


def start(place, owner_table, momentum, grad, planes, devices, chunks=8):
    mats, rows, cols = momentum.shape
    while mats % chunks:
        chunks -= 1
    hbm = pl.BlockSpec(memory_space=pltpu.HBM)
    outgoing = (devices, rows, cols)
    return pl.pallas_call(
        functools.partial(start_kernel, planes),
        grid_spec=pltpu.PrefetchScalarGridSpec(
            num_scalar_prefetch=1,
            grid=(1,),
            in_specs=[pl.BlockSpec((1, mats), lambda *_: (0, 0)), hbm, hbm],
            out_specs=[
                pl.BlockSpec((TABLE_ROWS, devices), lambda *_: (0, 0)),
                hbm,
                pl.BlockSpec(outgoing, lambda *_: (0, 0, 0)),
            ],
            scratch_shapes=[
                pltpu.VMEM(momentum.shape, momentum.dtype),
                pltpu.VMEM(grad.shape, grad.dtype),
                pltpu.SMEM((8, devices), jnp.int32),
                pltpu.SemaphoreType.DMA((2, chunks)),
                pltpu.SemaphoreType.DMA((chunks,)),
                pltpu.SemaphoreType.DMA,
            ],
        ),
        out_shape=[
            jax.ShapeDtypeStruct((TABLE_ROWS, devices), jnp.int32),
            jax.ShapeDtypeStruct(momentum.shape, jnp.float32),
            jax.ShapeDtypeStruct(outgoing, jnp.bfloat16),
        ],
        compiler_params=pltpu.CompilerParams(vmem_limit_bytes=60 * 1024 * 1024),
        name="start",
    )(place, owner_table.reshape(1, mats), momentum, grad)


def orthogonalize_kernel(scale, x_ref, out_ref, again_ref, iterate_ref, gram_ref, poly_ref):
    rows, cols = x_ref.shape
    tile, side = min(256, rows), min(256, cols) if cols % 256 == 0 else 128
    f32, bf16 = jnp.float32, jnp.bfloat16
    starts = range(0, cols, side)

    def put(ref, i, block):
        ref[i : i + side, i:] = block
        for j in range(i + side, cols, side):
            ref[j : j + side, i : i + side] = block[:, j - i : j - i + side].T

    def gram_rows(ref, i):
        return lax.dot_general(ref[:, i : i + side], ref[:, i:], (((0,), (0,)), ((), ())), preferred_element_type=f32)

    def poly():
        for i in starts:
            square = jnp.dot(gram_ref[i : i + side, :], gram_ref[:, i:], preferred_element_type=f32)
            put(poly_ref, i, (quintic_two * gram_ref[i : i + side, i:].astype(f32) + quintic_three * square).astype(bf16))

    def apply(source_ref, target_ref, factor, last):
        for i in range(0, rows, tile):
            part = source_ref[i : i + tile, :]
            step = quintic_one * part.astype(f32) + jnp.dot(part, poly_ref[...], preferred_element_type=f32)
            step = (step * factor).astype(bf16) if factor is not None else step.astype(bf16)
            step = step * jnp.asarray(scale, bf16) if last else step
            target_ref[i : i + tile, :] = step
            if last:
                again_ref[i : i + tile, :] = step

    gram = [gram_rows(x_ref, i) for i in starts]
    diagonal = lax.broadcasted_iota(jnp.int32, (side, side), 0) == lax.broadcasted_iota(jnp.int32, (side, side), 1)
    squares = sum(jnp.where(diagonal, block[:, :side], 0.0) for block in gram)
    trace = jnp.sum(jnp.sum(squares, axis=0, keepdims=True), axis=1, keepdims=True)
    factor = 1.0 / (jnp.sqrt(trace) + norm_epsilon)
    for i, block in zip(starts, gram):
        put(gram_ref, i, (block * factor * factor).astype(bf16))
    poly()
    apply(x_ref, iterate_ref, factor, False)
    for step in range(1, ITERS):
        for i in starts:
            put(gram_ref, i, gram_rows(iterate_ref, i).astype(bf16))
        poly()
        apply(iterate_ref, out_ref, None, True)


def orthogonalize(matrix, scale):
    rows, cols = matrix.shape
    return pl.pallas_call(
        functools.partial(orthogonalize_kernel, scale),
        out_shape=[jax.ShapeDtypeStruct((rows, cols), jnp.bfloat16)] * 2,
        scratch_shapes=[
            pltpu.VMEM((rows, cols), jnp.bfloat16),
            pltpu.VMEM((cols, cols), jnp.bfloat16),
            pltpu.VMEM((cols, cols), jnp.bfloat16),
        ],
        compiler_params=pltpu.CompilerParams(vmem_limit_bytes=24 * 1024 * 1024),
        cost_estimate=pl.CostEstimate(flops=ITERS * 2 * cols * cols * (2 * rows + cols), bytes_accessed=4 * rows * cols, transcendentals=0),
        name="orthogonalize",
    )(matrix)


def pack_kernel(table_ref, parts_ref, early_ref, out_ref):
    count, rows, _ = parts_ref.shape
    out_ref[:, rows:, :] = early_ref[...]

    def each(i, _):
        out_ref[i, :rows, :] = parts_ref[table_ref[PART, i]]

    lax.fori_loop(0, count, each, None, unroll=True)


def pack(table, parts, early):
    count, rows, cols = parts.shape
    shape = (count, rows + early.shape[1], cols)
    return pl.pallas_call(
        pack_kernel,
        grid_spec=pltpu.PrefetchScalarGridSpec(
            num_scalar_prefetch=1,
            grid=(1,),
            in_specs=[pl.BlockSpec(x.shape, lambda *_: (0, 0, 0)) for x in (parts, early)],
            out_specs=pl.BlockSpec(shape, lambda *_: (0, 0, 0)),
        ),
        out_shape=jax.ShapeDtypeStruct(shape, parts.dtype),
        compiler_params=pltpu.CompilerParams(vmem_limit_bytes=14 * 1024 * 1024),
        name="pack",
    )(table, parts, early)


def spread(table_ref, first, pieces, staged_ref, update_ref, sem):
    for k, piece in enumerate(pieces):
        count = piece.shape[0]
        staged_ref[k * count : (k + 1) * count] = piece.astype(jnp.float32)

        def each(i, _, at=k * count):
            matrix = table_ref[MATRIX, first * count + at + i]

            @pl.when(matrix >= 0)
            def _():
                pltpu.make_async_copy(staged_ref.at[at + i], update_ref.at[matrix], sem).start()

        lax.fori_loop(0, count, each, None, unroll=8 if count % 8 == 0 else 1)


def finish_kernel(pieces, early, table_ref, place_ref, mine_ref, second_ref, *refs):
    pieces_refs, (update_ref, owned_ref, staged_ref, slots_ref, sem, slot_sem) = refs[:pieces], refs[pieces:]
    me = place_ref[1]
    count, rows, cols = pieces_refs[0].shape
    whole_rows = mine_ref.shape[0]
    mine = mine_ref[...]
    slots_ref[0] = jnp.where(table_ref[FIRST, me] > 0, mine, jnp.zeros_like(mine))
    keep = second_ref.shape[1] - early * rows
    second = second_ref[:, :keep, :].reshape(whole_rows, cols)
    slots_ref[1] = jnp.where(table_ref[SECOND, me] > 0, second, jnp.zeros_like(second))
    owned = pltpu.make_async_copy(slots_ref, owned_ref, slot_sem)
    owned.start()
    early_rows = second_ref[:, keep:, :].astype(jnp.float32)
    values = [ref[...] for ref in pieces_refs] + [early_rows[:, i * rows : (i + 1) * rows, :] for i in range(early)]
    spread(table_ref, 0, values, staged_ref, update_ref, sem)
    pltpu.make_async_copy(staged_ref.at[pl.ds(0, update_ref.shape[0])], update_ref, sem).wait()
    owned.wait()


def finish(table, place, late, mine, second, mats, early):
    count, rows, cols = late[0].shape
    hbm = pl.BlockSpec(memory_space=pltpu.HBM)

    def whole(x):
        return pl.BlockSpec(x.shape, lambda *_: (0,) * len(x.shape))

    owned_shape = (CAP, *mine.shape)
    return pl.pallas_call(
        functools.partial(finish_kernel, len(late), early),
        grid_spec=pltpu.PrefetchScalarGridSpec(
            num_scalar_prefetch=2,
            grid=(1,),
            in_specs=[whole(mine), whole(second), *(whole(piece) for piece in late)],
            out_specs=[hbm, hbm],
            scratch_shapes=[
                pltpu.VMEM(((len(late) + early) * count, rows, cols), jnp.float32),
                pltpu.VMEM(owned_shape, mine.dtype),
                pltpu.SemaphoreType.DMA,
                pltpu.SemaphoreType.DMA,
            ],
        ),
        out_shape=[
            jax.ShapeDtypeStruct((mats, rows, cols), jnp.float32),
            jax.ShapeDtypeStruct(owned_shape, mine.dtype),
        ],
        compiler_params=pltpu.CompilerParams(vmem_limit_bytes=32 * 1024 * 1024),
        name="finish",
    )(table, place, mine, second, *late)


def spilled_kernel(table_ref, arrived_ref, out_ref):
    def each(i, _):
        out_ref[i] = arrived_ref[table_ref[HELPER_INDEX, i]]

    lax.fori_loop(0, out_ref.shape[0], each, None)


def spilled_rows(table, arrived):
    whole = pl.BlockSpec(arrived.shape, lambda *_: (0, 0, 0))
    return pl.pallas_call(
        spilled_kernel,
        grid_spec=pltpu.PrefetchScalarGridSpec(num_scalar_prefetch=1, grid=(1,), in_specs=[whole], out_specs=whole),
        out_shape=jax.ShapeDtypeStruct(arrived.shape, arrived.dtype),
        compiler_params=pltpu.CompilerParams(vmem_limit_bytes=14 * 1024 * 1024),
        name="spilled",
    )(table, arrived)


def send_planes(rows, way):
    planes = lax.axis_size("owner")
    me = lax.axis_index("owner")
    arrived = []
    for far in way:
        piece = lax.dynamic_index_in_dim(rows, lax.rem(me + far, planes), 1, keepdims=False)
        arrived.append(lax.ppermute(piece, "owner", [(i, (i + far) % planes) for i in range(planes)]) if far else piece)
    return arrived


def shards(momentum, grad, owner_table):
    dp_count = lax.axis_size("dp")
    planes = lax.axis_size("owner")
    devices = dp_count * planes
    mats, rows, cols = momentum.shape
    whole_rows = devices * rows
    early_ways = early_distances(planes)
    my_plane = lax.axis_index("owner")
    place = jnp.stack([my_plane, lax.axis_index("dp") * planes + my_plane]).astype(jnp.int32)
    with jax.named_scope("start"):
        table, new_momentum, outgoing = start(place, owner_table, momentum, grad, planes, devices)
    with jax.named_scope("gather_matrix"):
        received = lax.all_to_all(outgoing, ("dp", "owner"), 0, 0, tiled=True)
        matrix = received.reshape(whole_rows, cols)
    with jax.named_scope("orthogonalize"):
        mine, again = orthogonalize(matrix, math.sqrt(whole_rows))
    with jax.named_scope("return_dp"):
        parts = lax.all_to_all(mine.reshape(dp_count, planes * rows, cols), "dp", 0, 0, tiled=True)
    with jax.named_scope("return_owner_early"):
        early = jnp.concatenate(send_planes(again.reshape(dp_count, planes, rows, cols), early_ways), 1)
    with jax.named_scope("return_owner"):
        late = send_planes(parts.reshape(dp_count, planes, rows, cols), [0, *late_distances(planes)])
    with jax.named_scope("second_matrix"):
        second = lax.all_to_all(pack(table, parts, early), "dp", 0, 0, tiled=True)

    def with_spilled(second, *late):
        came_early = second[:, planes * rows :].reshape(dp_count, len(early_ways), rows, cols)
        arrived = jnp.concatenate([*late, *(came_early[:, i] for i in range(len(early_ways)))])
        rows_out = lax.all_to_all(spilled_rows(table, arrived), ("dp", "owner"), 0, 0, tiled=True)
        return jnp.concatenate([rows_out.reshape(dp_count, planes * rows, cols), second[:, planes * rows :]], 1)

    with jax.named_scope("spilled"):
        second = lax.cond(table[SPILLED, 0] > 0, with_spilled, lambda second, *late: second, second, *late)
    with jax.named_scope("finish"):
        update, owned = finish(table, place, late, mine, second, mats, len(early_ways))
    return new_momentum, update, owned[:, None]


def solution(mesh):
    in_specs = (P(None, ("dp", "owner"), None), P(None, ("dp", "owner"), None), P())
    out_specs = (
        P(None, ("dp", "owner"), None),
        P(None, ("dp", "owner"), None),
        P(None, ("dp", "owner"), None, None),
    )
    return jax.shard_map(shards, mesh=mesh, in_specs=in_specs, out_specs=out_specs, check_vma=False)
```

```python
import functools
import math

import jax
import jax.numpy as jnp
from jax import lax
from jax.experimental import pallas as pl
from jax.experimental.pallas import tpu as pltpu
from jax.sharding import PartitionSpec as P

ITERS = 2
CAP = 2

momentum_decay = 0.95
quintic_one = 3.4445
quintic_two = -4.775
quintic_three = 2.0315
norm_epsilon = 1e-07

SLOT, FIRST, SECOND, SPILLED, PART, MATRIX, HELPER_INDEX = range(7)
TABLE_ROWS = 8


def early_distances(planes):
    return [planes // 2 - 1, planes // 2 + 1]


def late_distances(planes):
    early = early_distances(planes)
    return sorted((far for far in range(1, planes) if far not in early), key=lambda far: -min(far, planes - far))


def distances(planes):
    return [0, *late_distances(planes), *early_distances(planes)]


def fill_table(planes, owner_ref, table_ref):
    mats = owner_ref.shape[1]
    devices = table_ref.shape[1]
    my_plane = lax.axis_index("owner")
    f32 = jnp.float32

    def iota(rows, cols, axis):
        return lax.broadcasted_iota(jnp.int32, (rows, cols), axis)

    def total(cond, axis):
        return jnp.sum(jnp.where(cond, 1.0, 0.0).astype(f32), axis=axis, keepdims=True)

    def column(row):
        n = row.shape[1]
        return jnp.sum(jnp.where(iota(n, n, 0) == iota(n, n, 1), row, 0.0), axis=1, keepdims=True)

    own_row = owner_ref[...].astype(f32)
    own_col = column(own_row)
    same = own_col == own_row
    rank_row = total(same & (iota(mats, mats, 0) < iota(mats, mats, 1)), 0)
    rank_col = total(same & (iota(mats, mats, 1) < iota(mats, mats, 0)), 1)
    held = own_col == iota(mats, devices, 1).astype(f32)
    first_row = total(held & (rank_col == 0.0), 0)
    second_row = total(held & (rank_col == 1.0), 0)
    held = own_row == iota(devices, mats, 0).astype(f32)
    first_col = total(held & (rank_row == 0.0), 1)
    second_col = total(held & (rank_row == 1.0), 1)
    up, down = iota(devices, devices, 0), iota(devices, devices, 1)
    plane = (up & (planes - 1)) == (down & (planes - 1))
    before_row, before_col = up < down, down < up
    free_index = total(before_col & plane & (first_row == 0.0), 1)
    second_index = total(before_row & plane & (second_col == 1.0), 0)
    pair = plane & (first_col == 0.0) & (second_row == 1.0) & (free_index == second_index)
    left_row = second_row - total(pair, 0)
    idle_col = 1.0 - first_col - total(pair, 1)
    left_col = column(left_row)
    idle_row = jnp.sum(jnp.where(up == down, idle_col, 0.0), axis=0, keepdims=True)
    left_index = total(before_row & (left_col == 1.0), 0)
    idle_index = total(before_col & (idle_row == 1.0), 1)
    spill = (left_row == 1.0) & (idle_col == 1.0) & (left_index == idle_index)
    helper_row = jnp.sum(jnp.where(pair | spill, up.astype(f32), 0.0), axis=0, keepdims=True)
    helper_col = column(helper_row)
    helper_of = jnp.sum(jnp.where(held, helper_col, 0.0), axis=0, keepdims=True)
    slot_row = jnp.where(rank_row == 0.0, own_row, helper_of)
    spilled = jnp.sum(left_row, axis=1, keepdims=True)
    slot_row = slot_row.astype(jnp.int32)
    helper_row = helper_row.astype(jnp.int32)
    shift = planes.bit_length() - 1
    count = devices // planes

    order = distances(planes)

    def arrival(slot):
        far = (my_plane - slot) & (planes - 1)
        position = sum(jnp.where(far == distance, i, 0) for i, distance in enumerate(order))
        return position * count + (slot >> shift)

    slot_col = column(slot_row.astype(f32)).astype(jnp.int32)
    lands = arrival(slot_col) == iota(mats, devices, 1)
    matrix_row = jnp.sum(jnp.where(lands, iota(mats, devices, 0) + 1, 0).astype(f32), axis=0, keepdims=True) - 1.0

    mine = up == (down * planes + my_plane)
    helper_here = column(helper_row.astype(f32))
    part_row = jnp.sum(jnp.where(mine, helper_here, 0.0), axis=0, keepdims=True).astype(jnp.int32) >> shift

    def put(row, values):
        table_ref[row : row + 1, : values.shape[1]] = values.astype(jnp.int32)

    table_ref[...] = jnp.zeros_like(table_ref)
    put(SLOT, slot_row)
    put(FIRST, first_row)
    put(SECOND, second_row)
    put(SPILLED, jnp.broadcast_to(spilled, (1, devices)))
    put(PART, part_row)
    put(MATRIX, matrix_row)
    put(HELPER_INDEX, arrival(helper_row))


def start_kernel(
    planes, owner_ref, momentum_ref, grad_ref, table_ref, new_ref, out_ref, new, grad, slots, in_sem, out_sem, slot_sem
):
    chunks = in_sem.shape[1]
    block = new.shape[0] // chunks

    def part(chunk):
        return pl.ds(chunk * block, block)

    def copies_in(chunk):
        return (
            pltpu.make_async_copy(momentum_ref.at[part(chunk)], new.at[part(chunk)], in_sem.at[0, chunk]),
            pltpu.make_async_copy(grad_ref.at[part(chunk)], grad.at[part(chunk)], in_sem.at[1, chunk]),
        )

    def copy_out(chunk):
        return pltpu.make_async_copy(new.at[part(chunk)], new_ref.at[part(chunk)], out_sem.at[chunk])

    for chunk in range(chunks):
        for copy in copies_in(chunk):
            copy.start()
    fill_table(planes, owner_ref, table_ref)
    slot_copy = pltpu.make_async_copy(table_ref.at[pl.ds(0, 8)], slots, slot_sem)
    slot_copy.start()
    slot_copy.wait()

    def each(chunk, _):
        for copy in copies_in(chunk):
            copy.wait()
        for i in range(block):
            mat = chunk * block + i
            value = grad[mat].astype(jnp.float32)
            result = momentum_decay * new[mat] + value
            new[mat] = result
            out_ref[slots[SLOT, mat]] = (value + momentum_decay * result).astype(out_ref.dtype)
        copy_out(chunk).start()

    lax.fori_loop(0, chunks, each, None)
    for chunk in range(chunks):
        copy_out(chunk).wait()


def start(owner_table, momentum, grad, planes, devices, chunks=8):
    mats, rows, cols = momentum.shape
    while mats % chunks:
        chunks -= 1
    hbm = pl.BlockSpec(memory_space=pltpu.HBM)
    outgoing = (devices, rows, cols)
    return pl.pallas_call(
        functools.partial(start_kernel, planes),
        grid_spec=pltpu.PrefetchScalarGridSpec(
            num_scalar_prefetch=0,
            grid=(1,),
            in_specs=[pl.BlockSpec((1, mats), lambda *_: (0, 0)), hbm, hbm],
            out_specs=[
                pl.BlockSpec((TABLE_ROWS, devices), lambda *_: (0, 0)),
                hbm,
                pl.BlockSpec(outgoing, lambda *_: (0, 0, 0)),
            ],
            scratch_shapes=[
                pltpu.VMEM(momentum.shape, momentum.dtype),
                pltpu.VMEM(grad.shape, grad.dtype),
                pltpu.SMEM((8, devices), jnp.int32),
                pltpu.SemaphoreType.DMA((2, chunks)),
                pltpu.SemaphoreType.DMA((chunks,)),
                pltpu.SemaphoreType.DMA,
            ],
        ),
        out_shape=[
            jax.ShapeDtypeStruct((TABLE_ROWS, devices), jnp.int32),
            jax.ShapeDtypeStruct(momentum.shape, jnp.float32),
            jax.ShapeDtypeStruct(outgoing, jnp.bfloat16),
        ],
        compiler_params=pltpu.CompilerParams(vmem_limit_bytes=60 * 1024 * 1024),
        name="start",
    )(owner_table.reshape(1, mats), momentum, grad)


def orthogonalize_kernel(scale, x_ref, out_ref, again_ref, iterate_ref, gram_ref, poly_ref):
    rows, cols = x_ref.shape
    tile, side = min(256, rows), min(256, cols) if cols % 256 == 0 else 128
    f32, bf16 = jnp.float32, jnp.bfloat16
    starts = range(0, cols, side)

    def put(ref, i, block):
        ref[i : i + side, i:] = block
        for j in range(i + side, cols, side):
            ref[j : j + side, i : i + side] = block[:, j - i : j - i + side].T

    def gram_rows(ref, i):
        return lax.dot_general(ref[:, i : i + side], ref[:, i:], (((0,), (0,)), ((), ())), preferred_element_type=f32)

    def poly():
        for i in starts:
            square = jnp.dot(gram_ref[i : i + side, :], gram_ref[:, i:], preferred_element_type=f32)
            put(poly_ref, i, (quintic_two * gram_ref[i : i + side, i:].astype(f32) + quintic_three * square).astype(bf16))

    def apply(source_ref, target_ref, factor, last):
        for i in range(0, rows, tile):
            part = source_ref[i : i + tile, :]
            step = quintic_one * part.astype(f32) + jnp.dot(part, poly_ref[...], preferred_element_type=f32)
            step = (step * factor).astype(bf16) if factor is not None else step.astype(bf16)
            step = step * jnp.asarray(scale, bf16) if last else step
            target_ref[i : i + tile, :] = step
            if last:
                again_ref[i : i + tile, :] = step

    gram = [gram_rows(x_ref, i) for i in starts]
    diagonal = lax.broadcasted_iota(jnp.int32, (side, side), 0) == lax.broadcasted_iota(jnp.int32, (side, side), 1)
    squares = sum(jnp.where(diagonal, block[:, :side], 0.0) for block in gram)
    trace = jnp.sum(jnp.sum(squares, axis=0, keepdims=True), axis=1, keepdims=True)
    factor = 1.0 / (jnp.sqrt(trace) + norm_epsilon)
    for i, block in zip(starts, gram):
        put(gram_ref, i, (block * factor * factor).astype(bf16))
    poly()
    apply(x_ref, iterate_ref, factor, False)
    for step in range(1, ITERS):
        for i in starts:
            put(gram_ref, i, gram_rows(iterate_ref, i).astype(bf16))
        poly()
        apply(iterate_ref, out_ref, None, True)


def orthogonalize(matrix, scale):
    rows, cols = matrix.shape
    return pl.pallas_call(
        functools.partial(orthogonalize_kernel, scale),
        out_shape=[jax.ShapeDtypeStruct((rows, cols), jnp.bfloat16)] * 2,
        scratch_shapes=[
            pltpu.VMEM((rows, cols), jnp.bfloat16),
            pltpu.VMEM((cols, cols), jnp.bfloat16),
            pltpu.VMEM((cols, cols), jnp.bfloat16),
        ],
        compiler_params=pltpu.CompilerParams(vmem_limit_bytes=24 * 1024 * 1024),
        cost_estimate=pl.CostEstimate(flops=ITERS * 2 * cols * cols * (2 * rows + cols), bytes_accessed=4 * rows * cols, transcendentals=0),
        name="orthogonalize",
    )(matrix)


def pack_kernel(table_ref, parts_ref, *refs):
    early_refs, out_ref = refs[:-1], refs[-1]
    block = out_ref.shape[0]
    groups = parts_ref.shape[1]
    first = pl.program_id(0) * block
    for k, early_ref in enumerate(early_refs):
        out_ref[:, groups + k] = early_ref[...]
    for i in range(block):
        out_ref[i, :groups] = parts_ref[table_ref[PART, first + i]]


def pack(table, parts, early, steps=4):
    count, groups, rows, cols = parts.shape
    block = count // steps
    shape = (count, groups + len(early), rows, cols)
    return pl.pallas_call(
        pack_kernel,
        grid_spec=pltpu.PrefetchScalarGridSpec(
            num_scalar_prefetch=1,
            grid=(steps,),
            in_specs=[
                pl.BlockSpec(parts.shape, lambda i, *_: (0, 0, 0, 0)),
                *(pl.BlockSpec((block, rows, cols), lambda i, *_: (i, 0, 0)) for _ in early),
            ],
            out_specs=pl.BlockSpec((block, *shape[1:]), lambda i, *_: (i, 0, 0, 0)),
        ),
        out_shape=jax.ShapeDtypeStruct(shape, parts.dtype),
        compiler_params=pltpu.CompilerParams(vmem_limit_bytes=14 * 1024 * 1024),
        name="pack",
    )(table, parts, *early)


def finish_kernel(late, table_ref, mine_ref, second_ref, early_ref, *refs):
    late_refs, (update_ref, owned_ref, staged_ref, zero_ref, sem, owned_sem) = refs[:late], refs[late:]
    me = lax.axis_index("dp") * lax.axis_size("owner") + lax.axis_index("owner")
    tile = zero_ref.shape[0]
    zero_ref[...] = jnp.zeros_like(zero_ref)

    def owned(act):
        for slot, source_ref in enumerate((mine_ref, second_ref)):
            present = table_ref[FIRST + slot, me] > 0

            @pl.when(present)
            def _():
                act(pltpu.make_async_copy(source_ref, owned_ref.at[slot], owned_sem.at[slot, 0]))

            @pl.when(jnp.logical_not(present))
            def _():
                for i in range(source_ref.shape[0] // tile):
                    to_ref = owned_ref.at[slot, pl.ds(i * tile, tile)]
                    act(pltpu.make_async_copy(zero_ref, to_ref, owned_sem.at[slot, i]))

    owned(lambda copy: copy.start())
    count = early_ref.shape[0]
    pieces = [lambda ref=ref: ref[...] for ref in late_refs]
    pieces += [lambda k=k: early_ref[:, k] for k in range(early_ref.shape[1])]
    for k, piece in enumerate(pieces):
        staged_ref[k * count : (k + 1) * count] = piece().astype(jnp.float32)

        def each(i, _, at=k * count):
            matrix = table_ref[MATRIX, at + i]

            @pl.when(matrix >= 0)
            def _():
                pltpu.make_async_copy(staged_ref.at[at + i], update_ref.at[matrix], sem).start()

        lax.fori_loop(0, count, each, None, unroll=8 if count % 8 == 0 else 1)
    pltpu.make_async_copy(staged_ref.at[pl.ds(0, update_ref.shape[0])], update_ref, sem).wait()
    owned(lambda copy: copy.wait())


def finish(table, late, mine, second, packed, mats):
    count, rows, cols = late[0].shape
    groups, early = packed.shape[1], packed.shape[1] - second.shape[0] // (count * rows)
    hbm = pl.BlockSpec(memory_space=pltpu.HBM)
    tile = min(256, mine.shape[0])

    def whole(x):
        return pl.BlockSpec(x.shape, lambda *_: (0,) * len(x.shape))

    owned_shape = (CAP, *mine.shape)
    return pl.pallas_call(
        functools.partial(finish_kernel, len(late)),
        grid_spec=pltpu.PrefetchScalarGridSpec(
            num_scalar_prefetch=1,
            grid=(1,),
            in_specs=[
                whole(mine),
                whole(second),
                pl.BlockSpec((count, early, rows, cols), lambda *_: (0, groups // early - 1, 0, 0)),
                *(whole(piece) for piece in late),
            ],
            out_specs=[hbm, hbm],
            scratch_shapes=[
                pltpu.VMEM(((len(late) + early) * count, rows, cols), jnp.float32),
                pltpu.VMEM((tile, cols), mine.dtype),
                pltpu.SemaphoreType.DMA,
                pltpu.SemaphoreType.DMA((CAP, mine.shape[0] // tile)),
            ],
        ),
        out_shape=[
            jax.ShapeDtypeStruct((mats, rows, cols), jnp.float32),
            jax.ShapeDtypeStruct(owned_shape, mine.dtype),
        ],
        compiler_params=pltpu.CompilerParams(vmem_limit_bytes=24 * 1024 * 1024),
        name="finish",
    )(table, mine, second, packed, *late)


def spilled_kernel(table_ref, arrived_ref, out_ref):
    def each(i, _):
        out_ref[i] = arrived_ref[table_ref[HELPER_INDEX, i]]

    lax.fori_loop(0, out_ref.shape[0], each, None)


def spilled_rows(table, arrived):
    whole = pl.BlockSpec(arrived.shape, lambda *_: (0, 0, 0))
    return pl.pallas_call(
        spilled_kernel,
        grid_spec=pltpu.PrefetchScalarGridSpec(num_scalar_prefetch=1, grid=(1,), in_specs=[whole], out_specs=whole),
        out_shape=jax.ShapeDtypeStruct(arrived.shape, arrived.dtype),
        compiler_params=pltpu.CompilerParams(vmem_limit_bytes=14 * 1024 * 1024),
        name="spilled",
    )(table, arrived)


def send_planes(rows, way):
    planes = lax.axis_size("owner")
    me = lax.axis_index("owner")
    arrived = []
    for far in way:
        piece = lax.dynamic_index_in_dim(rows, lax.rem(me + far, planes), 1, keepdims=False)
        arrived.append(lax.ppermute(piece, "owner", [(i, (i + far) % planes) for i in range(planes)]) if far else piece)
    return arrived


def shards(momentum, grad, owner_table):
    dp_count = lax.axis_size("dp")
    planes = lax.axis_size("owner")
    devices = dp_count * planes
    mats, rows, cols = momentum.shape
    whole_rows = devices * rows
    with jax.named_scope("start"):
        table, new_momentum, outgoing = start(owner_table, momentum, grad, planes, devices)
    with jax.named_scope("gather_matrix"):
        received = lax.all_to_all(outgoing, ("dp", "owner"), 0, 0, tiled=True)
        matrix = received.reshape(whole_rows, cols)
    with jax.named_scope("orthogonalize"):
        mine, again = orthogonalize(matrix, math.sqrt(whole_rows))
    with jax.named_scope("return_dp"):
        groups = again.reshape(dp_count, planes, rows, cols)
        parts = lax.all_to_all(groups, "dp", 0, 0, tiled=True)
    with jax.named_scope("return_owner_early"):
        early = send_planes(groups, early_distances(planes))
    with jax.named_scope("return_owner"):
        late = send_planes(parts, [0, *late_distances(planes)])
    with jax.named_scope("second_matrix"):
        packed = lax.all_to_all(pack(table, parts, early), "dp", 0, 0, tiled=True)
        second = packed[:, :planes].reshape(whole_rows, cols)

    def with_spilled(second, packed, *late):
        arrived = jnp.concatenate([*late, *(packed[:, planes + i] for i in range(len(early)))])
        rows_out = lax.all_to_all(spilled_rows(table, arrived), ("dp", "owner"), 0, 0, tiled=True)
        return rows_out.reshape(whole_rows, cols)

    with jax.named_scope("spilled"):
        spilled = table[SPILLED, 0] > 0
        second = lax.cond(spilled, with_spilled, lambda second, *_: second, second, packed, *late)
    with jax.named_scope("finish"):
        update, owned = finish(table, late, mine, second, packed, mats)
    return new_momentum, update, owned[:, None]


def solution(mesh):
    in_specs = (P(None, ("dp", "owner"), None), P(None, ("dp", "owner"), None), P())
    out_specs = (
        P(None, ("dp", "owner"), None),
        P(None, ("dp", "owner"), None),
        P(None, ("dp", "owner"), None, None),
    )
    return jax.shard_map(shards, mesh=mesh, in_specs=in_specs, out_specs=out_specs, check_vma=False)
```

```python
import functools
import math

import jax
import jax.numpy as jnp
from jax import lax
from jax.experimental import pallas as pl
from jax.experimental.pallas import tpu as pltpu
from jax.sharding import PartitionSpec as P

ITERS = 2
CAP = 2

momentum_decay = 0.95
quintic_one = 3.4445
quintic_two = -4.775
quintic_three = 2.0315
norm_epsilon = 1e-07

SLOT, FIRST, SECOND, SPILLED, PART, MATRIX, HELPER_INDEX, HELPER = range(8)
TABLE_ROWS = 8


def early_distances(planes):
    return [planes // 2 - 1, planes // 2 + 1]


def late_distances(planes):
    early = early_distances(planes)
    return sorted((far for far in range(1, planes) if far not in early), key=lambda far: -min(far, planes - far))


def distances(planes):
    return [0, *late_distances(planes), *early_distances(planes)]


def fill_table(planes, owner_ref, table_ref):
    mats = owner_ref.shape[1]
    devices = table_ref.shape[1]
    my_plane = lax.axis_index("owner")
    f32 = jnp.float32

    def iota(rows, cols, axis):
        return lax.broadcasted_iota(jnp.int32, (rows, cols), axis)

    def total(cond, axis):
        return jnp.sum(jnp.where(cond, 1.0, 0.0).astype(f32), axis=axis, keepdims=True)

    def column(row):
        n = row.shape[1]
        return jnp.sum(jnp.where(iota(n, n, 0) == iota(n, n, 1), row, 0.0), axis=1, keepdims=True)

    own_row = owner_ref[...].astype(f32)
    own_col = column(own_row)
    same = own_col == own_row
    rank_row = total(same & (iota(mats, mats, 0) < iota(mats, mats, 1)), 0)
    rank_col = total(same & (iota(mats, mats, 1) < iota(mats, mats, 0)), 1)
    held = own_col == iota(mats, devices, 1).astype(f32)
    first_row = total(held & (rank_col == 0.0), 0)
    second_row = total(held & (rank_col == 1.0), 0)
    held = own_row == iota(devices, mats, 0).astype(f32)
    first_col = total(held & (rank_row == 0.0), 1)
    second_col = total(held & (rank_row == 1.0), 1)
    up, down = iota(devices, devices, 0), iota(devices, devices, 1)
    plane = (up & (planes - 1)) == (down & (planes - 1))
    before_row, before_col = up < down, down < up
    free_index = total(before_col & plane & (first_row == 0.0), 1)
    second_index = total(before_row & plane & (second_col == 1.0), 0)
    pair = plane & (first_col == 0.0) & (second_row == 1.0) & (free_index == second_index)
    left_row = second_row - total(pair, 0)
    spilled = jnp.sum(left_row, axis=1, keepdims=True)

    def put(row, values):
        table_ref[row : row + 1, : values.shape[1]] = values.astype(jnp.int32)

    def helpers(pairs):
        return jnp.sum(jnp.where(pairs, up.astype(f32), 0.0), axis=0, keepdims=True)

    table_ref[...] = jnp.zeros_like(table_ref)
    put(HELPER, helpers(pair))

    @pl.when(jnp.sum(left_row) > 0.0)
    def _():
        idle_col = 1.0 - first_col - total(pair, 1)
        left_col = column(left_row)
        idle_row = jnp.sum(jnp.where(up == down, idle_col, 0.0), axis=0, keepdims=True)
        left_index = total(before_row & (left_col == 1.0), 0)
        idle_index = total(before_col & (idle_row == 1.0), 1)
        put(HELPER, helpers(pair | ((left_row == 1.0) & (idle_col == 1.0) & (left_index == idle_index))))

    helper_row = table_ref[HELPER : HELPER + 1, :].astype(f32)
    helper_col = column(helper_row)
    helper_of = jnp.sum(jnp.where(held, helper_col, 0.0), axis=0, keepdims=True)
    slot_row = jnp.where(rank_row == 0.0, own_row, helper_of)
    slot_row = slot_row.astype(jnp.int32)
    helper_row = helper_row.astype(jnp.int32)
    shift = planes.bit_length() - 1
    count = devices // planes

    order = distances(planes)

    def arrival(slot):
        far = (my_plane - slot) & (planes - 1)
        position = sum(jnp.where(far == distance, i, 0) for i, distance in enumerate(order))
        return position * count + (slot >> shift)

    slot_col = column(slot_row.astype(f32)).astype(jnp.int32)
    lands = arrival(slot_col) == iota(mats, devices, 1)
    matrix_row = jnp.sum(jnp.where(lands, iota(mats, devices, 0) + 1, 0).astype(f32), axis=0, keepdims=True) - 1.0

    mine = up == (down * planes + my_plane)
    helper_here = column(helper_row.astype(f32))
    part_row = jnp.sum(jnp.where(mine, helper_here, 0.0), axis=0, keepdims=True).astype(jnp.int32) >> shift

    put(SLOT, slot_row)
    put(FIRST, first_row)
    put(SECOND, second_row)
    put(SPILLED, jnp.broadcast_to(spilled, (1, devices)))
    put(PART, part_row)
    put(MATRIX, matrix_row)
    put(HELPER_INDEX, arrival(helper_row))


def start_kernel(
    planes, owner_ref, momentum_ref, grad_ref, table_ref, new_ref, out_ref, new, grad, slots, in_sem, out_sem, slot_sem
):
    chunks = in_sem.shape[1]
    block = new.shape[0] // chunks

    def part(chunk):
        return pl.ds(chunk * block, block)

    def copies_in(chunk):
        return (
            pltpu.make_async_copy(momentum_ref.at[part(chunk)], new.at[part(chunk)], in_sem.at[0, chunk]),
            pltpu.make_async_copy(grad_ref.at[part(chunk)], grad.at[part(chunk)], in_sem.at[1, chunk]),
        )

    def copy_out(chunk):
        return pltpu.make_async_copy(new.at[part(chunk)], new_ref.at[part(chunk)], out_sem.at[chunk])

    for chunk in range(chunks):
        for copy in copies_in(chunk):
            copy.start()
    fill_table(planes, owner_ref, table_ref)
    slot_copy = pltpu.make_async_copy(table_ref.at[pl.ds(0, 8)], slots, slot_sem)
    slot_copy.start()
    slot_copy.wait()

    def each(chunk, _):
        for copy in copies_in(chunk):
            copy.wait()
        for i in range(block):
            mat = chunk * block + i
            value = grad[mat].astype(jnp.float32)
            result = momentum_decay * new[mat] + value
            new[mat] = result
            out_ref[slots[SLOT, mat]] = (value + momentum_decay * result).astype(out_ref.dtype)
        copy_out(chunk).start()

    lax.fori_loop(0, chunks, each, None)
    for chunk in range(chunks):
        copy_out(chunk).wait()


def start(owner_table, momentum, grad, planes, devices, chunks=8):
    mats, rows, cols = momentum.shape
    while mats % chunks:
        chunks -= 1
    hbm = pl.BlockSpec(memory_space=pltpu.HBM)
    outgoing = (devices, rows, cols)
    return pl.pallas_call(
        functools.partial(start_kernel, planes),
        grid_spec=pltpu.PrefetchScalarGridSpec(
            num_scalar_prefetch=0,
            grid=(1,),
            in_specs=[pl.BlockSpec((1, mats), lambda *_: (0, 0)), hbm, hbm],
            out_specs=[
                pl.BlockSpec((TABLE_ROWS, devices), lambda *_: (0, 0)),
                hbm,
                pl.BlockSpec(outgoing, lambda *_: (0, 0, 0)),
            ],
            scratch_shapes=[
                pltpu.VMEM(momentum.shape, momentum.dtype),
                pltpu.VMEM(grad.shape, grad.dtype),
                pltpu.SMEM((8, devices), jnp.int32),
                pltpu.SemaphoreType.DMA((2, chunks)),
                pltpu.SemaphoreType.DMA((chunks,)),
                pltpu.SemaphoreType.DMA,
            ],
        ),
        out_shape=[
            jax.ShapeDtypeStruct((TABLE_ROWS, devices), jnp.int32),
            jax.ShapeDtypeStruct(momentum.shape, jnp.float32),
            jax.ShapeDtypeStruct(outgoing, jnp.bfloat16),
        ],
        compiler_params=pltpu.CompilerParams(vmem_limit_bytes=60 * 1024 * 1024),
        name="start",
    )(owner_table.reshape(1, mats), momentum, grad)


def orthogonalize_kernel(scale, x_ref, out_ref, again_ref, iterate_ref, gram_ref, poly_ref, sem):
    rows, cols = x_ref.shape
    tile, side = min(256, rows), min(256, cols) if cols % 256 == 0 else 128
    f32, bf16 = jnp.float32, jnp.bfloat16
    starts = range(0, cols, side)

    def copy_out(i):
        return pltpu.make_async_copy(again_ref.at[pl.ds(i, tile)], out_ref.at[pl.ds(i, tile)], sem.at[i // tile])

    def put(ref, i, block):
        ref[i : i + side, i:] = block
        for j in range(i + side, cols, side):
            ref[j : j + side, i : i + side] = block[:, j - i : j - i + side].T

    def gram_rows(ref, i):
        return lax.dot_general(ref[:, i : i + side], ref[:, i:], (((0,), (0,)), ((), ())), preferred_element_type=f32)

    def poly():
        for i in starts:
            square = jnp.dot(gram_ref[i : i + side, :], gram_ref[:, i:], preferred_element_type=f32)
            put(poly_ref, i, (quintic_two * gram_ref[i : i + side, i:].astype(f32) + quintic_three * square).astype(bf16))

    def apply(source_ref, target_ref, factor, last):
        for i in range(0, rows, tile):
            part = source_ref[i : i + tile, :]
            step = quintic_one * part.astype(f32) + jnp.dot(part, poly_ref[...], preferred_element_type=f32)
            step = (step * factor).astype(bf16) if factor is not None else step.astype(bf16)
            step = step * jnp.asarray(scale, bf16) if last else step
            target_ref[i : i + tile, :] = step
            if last:
                copy_out(i).start()

    gram = [gram_rows(x_ref, i) for i in starts]
    diagonal = lax.broadcasted_iota(jnp.int32, (side, side), 0) == lax.broadcasted_iota(jnp.int32, (side, side), 1)
    squares = sum(jnp.where(diagonal, block[:, :side], 0.0) for block in gram)
    trace = jnp.sum(jnp.sum(squares, axis=0, keepdims=True), axis=1, keepdims=True)
    factor = 1.0 / (jnp.sqrt(trace) + norm_epsilon)
    for i, block in zip(starts, gram):
        put(gram_ref, i, (block * factor * factor).astype(bf16))
    poly()
    apply(x_ref, iterate_ref, factor, False)
    for step in range(1, ITERS):
        for i in starts:
            put(gram_ref, i, gram_rows(iterate_ref, i).astype(bf16))
        poly()
        apply(iterate_ref, again_ref, None, True)
    for i in range(0, rows, tile):
        copy_out(i).wait()


def orthogonalize(matrix, scale):
    rows, cols = matrix.shape
    return pl.pallas_call(
        functools.partial(orthogonalize_kernel, scale),
        out_shape=[jax.ShapeDtypeStruct((rows, cols), jnp.bfloat16)] * 2,
        out_specs=[pl.BlockSpec(memory_space=pltpu.HBM), pl.BlockSpec(memory_space=pltpu.VMEM)],
        scratch_shapes=[
            pltpu.VMEM((rows, cols), jnp.bfloat16),
            pltpu.VMEM((cols, cols), jnp.bfloat16),
            pltpu.VMEM((cols, cols), jnp.bfloat16),
            pltpu.SemaphoreType.DMA((rows // min(256, rows),)),
        ],
        compiler_params=pltpu.CompilerParams(vmem_limit_bytes=24 * 1024 * 1024),
        cost_estimate=pl.CostEstimate(flops=ITERS * 2 * cols * cols * (2 * rows + cols), bytes_accessed=4 * rows * cols, transcendentals=0),
        name="orthogonalize",
    )(matrix)


def pack_kernel(table_ref, parts_ref, early_ref, out_ref, sem):
    count, rows, _ = parts_ref.shape
    copies = [pltpu.make_async_copy(early_ref, out_ref.at[:, pl.ds(rows, early_ref.shape[1])], sem.at[count])]
    for i in range(count):
        to_ref = out_ref.at[i, pl.ds(0, rows)]
        copies.append(pltpu.make_async_copy(parts_ref.at[table_ref[PART, i]], to_ref, sem.at[i]))
    for copy in copies:
        copy.start()
    for copy in copies:
        copy.wait()


def pack(table, parts, early):
    count, rows, cols = parts.shape
    return pl.pallas_call(
        pack_kernel,
        grid_spec=pltpu.PrefetchScalarGridSpec(
            num_scalar_prefetch=1,
            grid=(1,),
            in_specs=[pl.BlockSpec(x.shape, lambda *_: (0, 0, 0)) for x in (parts, early)],
            out_specs=pl.BlockSpec(memory_space=pltpu.HBM),
            scratch_shapes=[pltpu.SemaphoreType.DMA((count + 1,))],
        ),
        out_shape=jax.ShapeDtypeStruct((count, rows + early.shape[1], cols), parts.dtype),
        compiler_params=pltpu.CompilerParams(vmem_limit_bytes=14 * 1024 * 1024),
        name="pack",
    )(table, parts, early)


def put_owned(table_ref, slot, copies, owned_ref, zero_ref, sem, act):
    me = lax.axis_index("dp") * lax.axis_size("owner") + lax.axis_index("owner")
    tile = zero_ref.shape[0]
    present = table_ref[FIRST + slot, me] > 0

    @pl.when(present)
    def _():
        for copy in copies:
            act(copy)

    @pl.when(jnp.logical_not(present))
    def _():
        for i in range(owned_ref.shape[1] // tile):
            act(pltpu.make_async_copy(zero_ref, owned_ref.at[slot, pl.ds(i * tile, tile)], sem.at[i]))


def put_rows(table_ref, position, rows, staged_ref, update_ref, sem):
    count = rows.shape[0]
    staged_ref[...] = rows.astype(jnp.float32)

    def each(i, _):
        matrix = table_ref[MATRIX, position + i]

        @pl.when(matrix >= 0)
        def _():
            pltpu.make_async_copy(staged_ref.at[i], update_ref.at[matrix], sem).start()

    lax.fori_loop(0, count, each, None, unroll=8 if count % 8 == 0 else 1)


def begin_kernel(table_ref, mine_ref, owned_ref, zero_ref, sem):
    zero_ref[...] = jnp.zeros_like(zero_ref)
    copy = pltpu.make_async_copy(mine_ref, owned_ref.at[0], sem.at[0])
    put_owned(table_ref, 0, [copy], owned_ref, zero_ref, sem, lambda copy: copy.start())
    put_owned(table_ref, 0, [copy], owned_ref, zero_ref, sem, lambda copy: copy.wait())


def begin(table, mine):
    hbm = pl.BlockSpec(memory_space=pltpu.HBM)
    rows, cols = mine.shape
    tile = min(256, rows)
    return pl.pallas_call(
        begin_kernel,
        grid_spec=pltpu.PrefetchScalarGridSpec(
            num_scalar_prefetch=1,
            grid=(1,),
            in_specs=[pl.BlockSpec((rows, cols), lambda *_: (0, 0))],
            out_specs=hbm,
            scratch_shapes=[pltpu.VMEM((tile, cols), mine.dtype), pltpu.SemaphoreType.DMA((rows // tile,))],
        ),
        out_shape=jax.ShapeDtypeStruct((CAP, rows, cols), mine.dtype),
        compiler_params=pltpu.CompilerParams(vmem_limit_bytes=8 * 1024 * 1024),
        cost_estimate=pl.CostEstimate(flops=0, bytes_accessed=4 * rows * cols, transcendentals=0),
        name="begin",
    )(table, mine)


def finish_kernel(late, table_ref, packed_ref, *refs):
    late_refs, refs = refs[:late], refs[late + 1 :]
    update_ref, owned_ref, staged_ref, zero_ref, sem, owned_sem = refs
    zero_ref[...] = jnp.zeros_like(zero_ref)
    count, rows, _ = late_refs[0].shape
    keep = owned_ref.shape[1] // count
    copies = [
        pltpu.make_async_copy(packed_ref.at[i, pl.ds(0, keep)], owned_ref.at[1, pl.ds(i * keep, keep)], owned_sem.at[i])
        for i in range(count)
    ]
    put_owned(table_ref, 1, copies, owned_ref, zero_ref, owned_sem, lambda copy: copy.start())
    early_rows = packed_ref[:, keep:, :].astype(jnp.float32)
    pieces = [lambda ref=ref: ref[...] for ref in late_refs]
    pieces += [lambda i=i: early_rows[:, i : i + rows, :] for i in range(0, early_rows.shape[1], rows)]
    for k, piece in enumerate(pieces):
        put_rows(table_ref, k * count, piece(), staged_ref.at[pl.ds(k * count, count)], update_ref, sem)
    put_owned(table_ref, 1, copies, owned_ref, zero_ref, owned_sem, lambda copy: copy.wait())

    pltpu.make_async_copy(staged_ref.at[pl.ds(0, update_ref.shape[0])], update_ref, sem).wait()


def finish(table, late, packed, owned, mats):
    count, rows, cols = late[0].shape
    early = packed.shape[1] // rows - owned.shape[1] // (count * rows)
    hbm = pl.BlockSpec(memory_space=pltpu.HBM)
    tile = min(256, owned.shape[1])

    def whole(x):
        return pl.BlockSpec(x.shape, lambda *_: (0,) * len(x.shape))

    return pl.pallas_call(
        functools.partial(finish_kernel, len(late)),
        grid_spec=pltpu.PrefetchScalarGridSpec(
            num_scalar_prefetch=1,
            grid=(1,),
            in_specs=[whole(packed), *(whole(piece) for piece in late), hbm],
            out_specs=[hbm, hbm],
            scratch_shapes=[
                pltpu.VMEM(((len(late) + early) * count, rows, cols), jnp.float32),
                pltpu.VMEM((tile, cols), owned.dtype),
                pltpu.SemaphoreType.DMA,
                pltpu.SemaphoreType.DMA((max(count, owned.shape[1] // tile),)),
            ],
        ),
        out_shape=[
            jax.ShapeDtypeStruct((mats, rows, cols), jnp.float32),
            jax.ShapeDtypeStruct(owned.shape, owned.dtype),
        ],
        input_output_aliases={2 + len(late): 1},
        compiler_params=pltpu.CompilerParams(vmem_limit_bytes=24 * 1024 * 1024),
        name="finish",
    )(table, packed, *late, owned)


def spilled_kernel(table_ref, arrived_ref, out_ref):
    def each(i, _):
        out_ref[i] = arrived_ref[table_ref[HELPER_INDEX, i]]

    lax.fori_loop(0, out_ref.shape[0], each, None)


def spilled_rows(table, arrived):
    whole = pl.BlockSpec(arrived.shape, lambda *_: (0, 0, 0))
    return pl.pallas_call(
        spilled_kernel,
        grid_spec=pltpu.PrefetchScalarGridSpec(num_scalar_prefetch=1, grid=(1,), in_specs=[whole], out_specs=whole),
        out_shape=jax.ShapeDtypeStruct(arrived.shape, arrived.dtype),
        compiler_params=pltpu.CompilerParams(vmem_limit_bytes=14 * 1024 * 1024),
        name="spilled",
    )(table, arrived)


def to_planes(rows, way):
    me, planes = lax.axis_index("owner"), lax.axis_size("owner")
    count = rows.shape[1] // planes
    return [lax.dynamic_slice_in_dim(rows, lax.rem(me + far, planes) * count, count, 1) for far in way]


def send(pieces, way):
    planes = lax.axis_size("owner")
    return [
        lax.ppermute(piece, "owner", [(i, (i + far) % planes) for i in range(planes)]) if far else piece
        for piece, far in zip(pieces, way)
    ]


def shards(momentum, grad, owner_table):
    dp_count = lax.axis_size("dp")
    planes = lax.axis_size("owner")
    devices = dp_count * planes
    mats, rows, cols = momentum.shape
    whole_rows = devices * rows

    with jax.named_scope("start"):
        table, new_momentum, outgoing = start(owner_table, momentum, grad, planes, devices)
    with jax.named_scope("gather_matrix"):
        received = lax.all_to_all(outgoing, ("dp", "owner"), 0, 0, tiled=True)
        matrix = received.reshape(whole_rows, cols)
    with jax.named_scope("orthogonalize"):
        mine, again = orthogonalize(matrix, math.sqrt(whole_rows))
    with jax.named_scope("return_dp"):
        parts = lax.all_to_all(mine.reshape(dp_count, planes * rows, cols), "dp", 0, 0, tiled=True)
    with jax.named_scope("return_owner_early"):
        way = early_distances(planes)
        early = jnp.concatenate(send(to_planes(again.reshape(dp_count, planes * rows, cols), way), way), 1)
    with jax.named_scope("return_owner"):
        way = [0, *late_distances(planes)]
        late = send(to_planes(parts, way), way)
    with jax.named_scope("second_matrix"):
        packed = lax.all_to_all(pack(table, parts, early), "dp", 0, 0, tiled=True)

    with jax.named_scope("begin"):
        owned = begin(table, mine)

    def with_spilled(packed, *late):
        came_early = packed[:, planes * rows :].reshape(dp_count, -1, rows, cols)
        arrived = jnp.concatenate([*late, *(came_early[:, i] for i in range(came_early.shape[1]))])
        rows_out = lax.all_to_all(spilled_rows(table, arrived), ("dp", "owner"), 0, 0, tiled=True)
        return jnp.concatenate([rows_out.reshape(dp_count, planes * rows, cols), packed[:, planes * rows :]], 1)

    with jax.named_scope("spilled"):
        packed = lax.cond(table[SPILLED, 0] > 0, with_spilled, lambda packed, *late: packed, packed, *late)
    with jax.named_scope("finish"):
        update, owned = finish(table, late, packed, owned, mats)
    return new_momentum, update, owned[:, None]


def solution(mesh):
    in_specs = (P(None, ("dp", "owner"), None), P(None, ("dp", "owner"), None), P())
    out_specs = (
        P(None, ("dp", "owner"), None),
        P(None, ("dp", "owner"), None),
        P(None, ("dp", "owner"), None, None),
    )
    return jax.shard_map(shards, mesh=mesh, in_specs=in_specs, out_specs=out_specs, check_vma=False)
```

```python
import functools
import math

import jax
import jax.numpy as jnp
from jax import lax
from jax.experimental import pallas as pl
from jax.experimental.pallas import tpu as pltpu
from jax.sharding import PartitionSpec as P

ITERS = 2
CAP = 2

momentum_decay = 0.95
quintic_one = 3.4445
quintic_two = -4.775
quintic_three = 2.0315
norm_epsilon = 1e-07

HOSTS, WAYS, WORK, OWNED, LEFT = 0, 16, 32, 40, 48
PLANES, COLUMNS, TABLE_ROWS = 8, 128, 56
HOST, MATRIX, LIST_ROWS = 0, 1, 8
FAR, ROUNDS = 63, 20


def chip_steps():
    steps = ([], [], [])
    for x in range(4):
        for y in range(4):
            for core, way in ((0, 1), (1, -1)):
                here = (x * 4 + y) * 2 + core
                steps[0].append((here, here + way))
                steps[1].append((here, ((x + way) % 4 * 4 + y) * 2 + core))
                steps[2].append((here, (x * 4 + (y + way) % 4) * 2 + core))
    return steps


def neighbours():
    lane = lax.broadcasted_iota(jnp.int32, (PLANES, COLUMNS), 1)
    core, y = lane & 1, (lane >> 1) & 3

    def at(values, way):
        return pltpu.roll(values, (COLUMNS - way) % COLUMNS, 1)

    def flip(values):
        return jnp.where(core == 0, at(values, 1), at(values, -1))

    def along_x(values, sign):
        return jnp.where(core == 0, at(values, 8 * sign), at(values, -8 * sign))

    def along_y(values, sign):
        up = jnp.where(y == 3, at(values, -6), at(values, 2))
        down = jnp.where(y == 0, at(values, 6), at(values, -2))
        return jnp.where((core == 0) == (sign > 0), up, down)

    pull = (flip, lambda values: along_x(values, -1), lambda values: along_y(values, -1))
    push = (flip, lambda values: along_x(values, 1), lambda values: along_y(values, 1))
    return pull, push


def search_turn(work, label, waiting):
    pull, push = neighbours()
    best, choice = jnp.full_like(work, FAR), jnp.zeros_like(work)
    for k in range(3):
        there = pull[k](label * 8 + work + 1)
        value = jnp.where((there & 7) == k + 2, FAR, there >> 3)
        choice = jnp.where(value < best, k + 1, choice)
        best = jnp.minimum(value, best)
    message = best * 8 + jnp.where(waiting > 0, choice, 0)
    moved = jnp.where(work == 0, best + 1, 0)
    taken = jnp.zeros_like(work)
    for k in range(3):
        there = push[k](message)
        moved = jnp.where(work == k + 1, (there >> 3) + 1, moved)
        taken = jnp.where((taken == 0) & ((there & 7) == k + 1), k + 1, taken)
    label = jnp.minimum(jnp.maximum(label, moved), FAR)
    waiting = waiting + jnp.where((taken > 0) & (work == 0), 1, 0)
    for k in range(3):
        waiting = waiting + pull[k](jnp.where((taken > 0) & (work == k + 1), 1, 0) - jnp.where(taken == k + 1, 1, 0))
    return jnp.where(taken > 0, taken, work), label, waiting


def search_rest(work, label, waiting):
    def going(state):
        count, _, _, _, left = state
        return (count < ROUNDS) & (left > 0)

    def turn(state):
        count, *found, _ = state
        found = search_turn(*search_turn(*found))
        return count + 2, *found, jnp.sum(found[2])

    _, work, _, _, left = lax.while_loop(going, turn, (jnp.int32(0), work, label, waiting, jnp.sum(waiting)))
    return work, left


def iota(rows, cols, axis):
    return lax.broadcasted_iota(jnp.int32, (rows, cols), axis)


def column(row):
    n = row.shape[1]
    return jnp.sum(jnp.where(iota(n, n, 0) == iota(n, n, 1), row, 0.0), axis=1, keepdims=True)


def count_owned(planes, owner_col):
    mats = owner_col.shape[0]
    owned = jnp.zeros((PLANES, COLUMNS), jnp.float32)
    index = (iota(mats, COLUMNS, 1) & 31) * planes
    for p in range(planes):
        hits = jnp.sum(jnp.where(owner_col == index + p, 1.0, 0.0), axis=0, keepdims=True)
        owned = jnp.where(iota(PLANES, COLUMNS, 0) == p, hits, owned)
    return owned.astype(jnp.int32)


def rank_of(owner_row, owner_col):
    mats = owner_col.shape[0]
    earlier = (owner_col == owner_row) & (iota(mats, mats, 1) < iota(mats, mats, 0))
    return jnp.sum(jnp.where(earlier, 1.0, 0.0), axis=1, keepdims=True).astype(jnp.int32)


def fill_lists(planes, owner_col, rank_col, table_ref, lists_ref):
    mats, devices = owner_col.shape[0], lists_ref.shape[1]
    shift = planes.bit_length() - 1
    at_dp = jnp.where(iota(mats, COLUMNS, 1) == owner_col >> shift, 1.0, 0.0)
    hosts = table_ref[HOSTS : HOSTS + CAP * PLANES, :].astype(jnp.float32)
    found = lax.dot_general(at_dp, hosts, (((1,), (1,)), ((), ())), preferred_element_type=jnp.float32)
    wanted = iota(mats, CAP * PLANES, 1) == rank_col * PLANES + (owner_col & (planes - 1))
    host_col = jnp.sum(jnp.where(wanted, found, 0.0), axis=1, keepdims=True)
    host_row = jnp.sum(jnp.where(iota(mats, mats, 0) == iota(mats, mats, 1), host_col, 0.0), axis=0, keepdims=True)
    here = host_col.astype(jnp.int32) == iota(mats, devices, 1)
    number = (iota(mats, devices, 0) + 1).astype(jnp.float32)
    matrix_row = jnp.sum(jnp.where(here, number, 0.0), axis=0, keepdims=True) - 1.0
    lists_ref[...] = jnp.zeros_like(lists_ref)
    lists_ref[HOST : HOST + 1, :mats] = host_row.astype(jnp.int32)
    lists_ref[MATRIX : MATRIX + 1, :] = matrix_row.astype(jnp.int32)


def fill_table(planes, owned, work, left, table_ref):
    plane, lane = (iota(PLANES, COLUMNS, axis) for axis in (0, 1))
    pull, _ = neighbours()
    device = (lane & 31) * planes + plane
    none = jnp.full_like(owned, -1)
    hosts, ways = [none, none], [none, none]
    options = [(work == 0, device, 0)] + [(pull[k](work) == k + 1, pull[k](device), k + 1) for k in range(3)]
    for chosen, host, way in options:
        for slot in (1, 0):
            free = hosts[slot] < 0 if slot == 0 else (hosts[1] < 0) & (hosts[0] >= 0)
            hosts[slot] = jnp.where(chosen & free, host, hosts[slot])
            ways[slot] = jnp.where(chosen & free, way, ways[slot])
    for slot in range(CAP):
        table_ref[HOSTS + slot * PLANES : HOSTS + (slot + 1) * PLANES, :] = hosts[slot]
        table_ref[WAYS + slot * PLANES : WAYS + (slot + 1) * PLANES, :] = ways[slot]
    table_ref[WORK : WORK + PLANES, :] = work
    table_ref[OWNED : OWNED + PLANES, :] = owned
    table_ref[LEFT : LEFT + PLANES, :] = jnp.zeros_like(owned) + left


def place_left(planes, devices, table_ref):
    shift = planes.bit_length() - 1

    def each(i, idle):
        device = i // CAP
        plane, dp = device & (planes - 1), device >> shift
        host_row = HOSTS + (i % CAP) * PLANES + plane
        alone = (table_ref[OWNED + plane, dp] > i % CAP) & (table_ref[host_row, dp] < 0)

        def find(at):
            return lax.while_loop(lambda at: table_ref[WORK + (at & (planes - 1)), at >> shift] >= 0, lambda at: at + 1, at)

        @pl.when(alone)
        def _():
            table_ref[host_row, dp] = find(idle)

        return lax.cond(alone, lambda: find(idle) + 1, lambda: idle)

    lax.fori_loop(0, CAP * devices, each, jnp.int32(0))


def start_kernel(
    planes, owner_ref, momentum_ref, grad_ref, table_ref, lists_ref, new_ref, out_ref,
    new, grad, fixed, hosts, in_sem, out_sem, table_sem, rows_sem
):
    chunks = in_sem.shape[1]
    block = new.shape[0] // chunks

    def part(chunk):
        return pl.ds(chunk * block, block)

    def copies_in(chunk):
        return (
            pltpu.make_async_copy(momentum_ref.at[part(chunk)], new.at[part(chunk)], in_sem.at[0, chunk]),
            pltpu.make_async_copy(grad_ref.at[part(chunk)], grad.at[part(chunk)], in_sem.at[1, chunk]),
        )

    def copy_out(chunk):
        return pltpu.make_async_copy(new.at[part(chunk)], new_ref.at[part(chunk)], out_sem.at[chunk])

    for chunk in range(chunks):
        for copy in copies_in(chunk):
            copy.start()
    owner_row = owner_ref[...]
    owner_col = column(owner_row.astype(jnp.float32)).astype(jnp.int32)
    owned = count_owned(planes, owner_col)
    rank_col = rank_of(owner_row, owner_col)

    def each_chunk(chunk, found):
        for copy in copies_in(chunk):
            copy.wait()
        for i in range(block):
            mat = chunk * block + i
            value = grad[mat].astype(jnp.float32)
            result = momentum_decay * new[mat] + value
            new[mat] = result
            grad[mat] = (value + momentum_decay * result).astype(grad.dtype)
        copy_out(chunk).start()
        return search_turn(*found)

    found = (jnp.where(owned > 0, 0, -1), jnp.where(owned > 0, 1, 0), jnp.maximum(owned - 1, 0))
    work, left = search_rest(*lax.fori_loop(0, chunks, each_chunk, found))
    fill_table(planes, owned, work, left, table_ref)

    @pl.when(left > 0)
    def _():
        copy = pltpu.make_async_copy(table_ref, fixed, table_sem)
        copy.start()
        copy.wait()
        place_left(planes, out_ref.shape[0], fixed)
        copy = pltpu.make_async_copy(fixed, table_ref, table_sem)
        copy.start()
        copy.wait()

    fill_lists(planes, owner_col, rank_col, table_ref, lists_ref)
    copy = pltpu.make_async_copy(lists_ref, hosts, table_sem)
    copy.start()
    copy.wait()

    def each(mat, _):
        pltpu.make_async_copy(grad.at[mat], out_ref.at[hosts[HOST, mat]], rows_sem).start()

    mats = new.shape[0]
    lax.fori_loop(0, mats, each, None, unroll=8 if mats % 8 == 0 else 1)
    pltpu.make_async_copy(grad, out_ref.at[pl.ds(0, mats)], rows_sem).wait()
    for chunk in range(chunks):
        copy_out(chunk).wait()


def start(owner_table, momentum, grad, planes, devices, chunks=6):
    mats, rows, cols = momentum.shape
    while mats % chunks:
        chunks -= 1
    hbm = pl.BlockSpec(memory_space=pltpu.HBM)
    outgoing = (devices, rows, cols)
    return pl.pallas_call(
        functools.partial(start_kernel, planes),
        grid=(1,),
        in_specs=[pl.BlockSpec((1, mats), lambda *_: (0, 0)), hbm, hbm],
        out_specs=[
            pl.BlockSpec((TABLE_ROWS, COLUMNS), lambda *_: (0, 0)),
            pl.BlockSpec((LIST_ROWS, devices), lambda *_: (0, 0)),
            hbm,
            hbm,
        ],
        scratch_shapes=[
            pltpu.VMEM(momentum.shape, momentum.dtype),
            pltpu.VMEM(grad.shape, grad.dtype),
            pltpu.SMEM((TABLE_ROWS, COLUMNS), jnp.int32),
            pltpu.SMEM((LIST_ROWS, devices), jnp.int32),
            pltpu.SemaphoreType.DMA((2, chunks)),
            pltpu.SemaphoreType.DMA((chunks,)),
            pltpu.SemaphoreType.DMA,
            pltpu.SemaphoreType.DMA,
        ],
        out_shape=[
            jax.ShapeDtypeStruct((TABLE_ROWS, COLUMNS), jnp.int32),
            jax.ShapeDtypeStruct((LIST_ROWS, devices), jnp.int32),
            jax.ShapeDtypeStruct(momentum.shape, jnp.float32),
            jax.ShapeDtypeStruct(outgoing, jnp.bfloat16),
        ],
        compiler_params=pltpu.CompilerParams(vmem_limit_bytes=60 * 1024 * 1024),
        name="start",
    )(owner_table.reshape(1, mats), momentum, grad)


def orthogonalize_kernel(scale, x_ref, out_ref, iterate_ref, gram_ref, poly_ref):
    rows, cols = x_ref.shape
    tile, side = min(256, rows), min(256, cols) if cols % 256 == 0 else 128
    f32, bf16 = jnp.float32, jnp.bfloat16
    starts = range(0, cols, side)

    def put(ref, i, block):
        ref[i : i + side, i:] = block
        for j in range(i + side, cols, side):
            ref[j : j + side, i : i + side] = block[:, j - i : j - i + side].T

    def gram_rows(ref, i):
        return lax.dot_general(ref[:, i : i + side], ref[:, i:], (((0,), (0,)), ((), ())), preferred_element_type=f32)

    def poly():
        for i in starts:
            square = jnp.dot(gram_ref[i : i + side, :], gram_ref[:, i:], preferred_element_type=f32)
            put(poly_ref, i, (quintic_two * gram_ref[i : i + side, i:].astype(f32) + quintic_three * square).astype(bf16))

    def apply(source_ref, target_ref, factor, last):
        for i in range(0, rows, tile):
            part = source_ref[i : i + tile, :]
            step = quintic_one * part.astype(f32) + jnp.dot(part, poly_ref[...], preferred_element_type=f32)
            step = (step * factor).astype(bf16) if factor is not None else step.astype(bf16)
            step = step * jnp.asarray(scale, bf16) if last else step
            target_ref[i : i + tile, :] = step

    gram = [gram_rows(x_ref, i) for i in starts]
    diagonal = lax.broadcasted_iota(jnp.int32, (side, side), 0) == lax.broadcasted_iota(jnp.int32, (side, side), 1)
    squares = sum(jnp.where(diagonal, block[:, :side], 0.0) for block in gram)
    trace = jnp.sum(jnp.sum(squares, axis=0, keepdims=True), axis=1, keepdims=True)
    factor = 1.0 / (jnp.sqrt(trace) + norm_epsilon)
    for i, block in zip(starts, gram):
        put(gram_ref, i, (block * factor * factor).astype(bf16))
    poly()
    apply(x_ref, iterate_ref, factor, False)
    for step in range(1, ITERS):
        for i in starts:
            put(gram_ref, i, gram_rows(iterate_ref, i).astype(bf16))
        poly()
        apply(iterate_ref, out_ref, None, True)


def orthogonalize(matrix, scale):
    rows, cols = matrix.shape
    return pl.pallas_call(
        functools.partial(orthogonalize_kernel, scale),
        out_shape=jax.ShapeDtypeStruct((rows, cols), jnp.bfloat16),
        scratch_shapes=[
            pltpu.VMEM((rows, cols), jnp.bfloat16),
            pltpu.VMEM((cols, cols), jnp.bfloat16),
            pltpu.VMEM((cols, cols), jnp.bfloat16),
        ],
        compiler_params=pltpu.CompilerParams(vmem_limit_bytes=24 * 1024 * 1024),
        cost_estimate=pl.CostEstimate(flops=ITERS * 2 * cols * cols * (2 * rows + cols), bytes_accessed=4 * rows * cols, transcendentals=0),
        name="orthogonalize",
    )(matrix)


def begin_kernel(table_ref, *refs):
    sources, (owned_ref, held_ref, sem) = refs[:-3], refs[-3:]
    plane, dp = lax.axis_index("owner"), lax.axis_index("dp")
    ways = [table_ref[WAYS + slot * PLANES + plane, dp] for slot in range(CAP)]

    def bring(act):
        for slot, way in enumerate(ways):
            for k, source in enumerate(sources):

                @pl.when(way == k)
                def _():
                    act(pltpu.make_async_copy(source, held_ref.at[slot], sem.at[slot]))

    bring(lambda copy: copy.start())
    for slot, way in enumerate(ways):

        @pl.when(way < 0)
        def _():
            held_ref[slot] = jnp.zeros_like(held_ref[slot])

    bring(lambda copy: copy.wait())
    copy = pltpu.make_async_copy(held_ref, owned_ref, sem.at[CAP])
    copy.start()
    copy.wait()


def begin(table, sources):
    hbm = pl.BlockSpec(memory_space=pltpu.HBM)
    shape = (CAP, *sources[0].shape)
    return pl.pallas_call(
        begin_kernel,
        grid_spec=pltpu.PrefetchScalarGridSpec(
            num_scalar_prefetch=1,
            grid=(1,),
            in_specs=[hbm] * len(sources),
            out_specs=hbm,
            scratch_shapes=[pltpu.VMEM(shape, jnp.bfloat16), pltpu.SemaphoreType.DMA((CAP + 1,))],
        ),
        out_shape=jax.ShapeDtypeStruct(shape, jnp.bfloat16),
        compiler_params=pltpu.CompilerParams(vmem_limit_bytes=8 * 1024 * 1024),
        cost_estimate=pl.CostEstimate(flops=0, bytes_accessed=4 * math.prod(shape), transcendentals=0),
        name="begin",
    )(table, *sources)


def finish_kernel(lists_ref, rows_ref, _, update_ref, owned_ref, staged_ref, sem):
    devices = rows_ref.shape[0]
    count = min(32, devices)

    def each(chunk, _):
        first = chunk * count
        staged_ref[pl.ds(first, count)] = rows_ref[pl.ds(first, count)].astype(jnp.float32)
        for i in range(count):
            matrix = lists_ref[MATRIX, first + i]

            @pl.when(matrix >= 0)
            def _():
                pltpu.make_async_copy(staged_ref.at[first + i], update_ref.at[matrix], sem).start()

    lax.fori_loop(0, devices // count, each, None)
    pltpu.make_async_copy(staged_ref.at[pl.ds(0, update_ref.shape[0])], update_ref, sem).wait()


def finish(lists, arrived, owned, mats):
    hbm = pl.BlockSpec(memory_space=pltpu.HBM)
    _, rows, cols = arrived.shape
    return pl.pallas_call(
        finish_kernel,
        grid_spec=pltpu.PrefetchScalarGridSpec(
            num_scalar_prefetch=1,
            grid=(1,),
            in_specs=[pl.BlockSpec(arrived.shape, lambda *_: (0, 0, 0)), hbm],
            out_specs=[hbm, hbm],
            scratch_shapes=[pltpu.VMEM(arrived.shape, jnp.float32), pltpu.SemaphoreType.DMA],
        ),
        out_shape=[
            jax.ShapeDtypeStruct((mats, rows, cols), jnp.float32),
            jax.ShapeDtypeStruct(owned.shape, owned.dtype),
        ],
        input_output_aliases={2: 1},
        compiler_params=pltpu.CompilerParams(vmem_limit_bytes=20 * 1024 * 1024),
        name="finish",
    )(lists, arrived, owned)


def left_kernel(planes, slot, table_ref, arrived_ref, out_ref):
    shift = planes.bit_length() - 1

    def each(i, _):
        host = table_ref[HOSTS + slot * PLANES + (i & (planes - 1)), i >> shift]
        out_ref[i] = arrived_ref[jnp.maximum(host, 0)]

    lax.fori_loop(0, out_ref.shape[0], each, None)


def left_rows(table, arrived, planes, slot):
    whole = pl.BlockSpec(arrived.shape, lambda *_: (0, 0, 0))
    return pl.pallas_call(
        functools.partial(left_kernel, planes, slot),
        grid_spec=pltpu.PrefetchScalarGridSpec(num_scalar_prefetch=1, grid=(1,), in_specs=[whole], out_specs=whole),
        out_shape=jax.ShapeDtypeStruct(arrived.shape, arrived.dtype),
        compiler_params=pltpu.CompilerParams(vmem_limit_bytes=14 * 1024 * 1024),
        name="left",
    )(table, arrived)


def shards(momentum, grad, owner_table):
    dp_count = lax.axis_size("dp")
    planes = lax.axis_size("owner")
    devices = dp_count * planes
    mats, rows, cols = momentum.shape
    whole_rows = devices * rows
    both = ("dp", "owner")
    with jax.named_scope("start"):
        table, lists, new_momentum, outgoing = start(owner_table, momentum, grad, planes, devices)
    with jax.named_scope("gather_matrix"):
        received = lax.all_to_all(outgoing, both, 0, 0, tiled=True)
        matrix = received.reshape(whole_rows, cols)
    with jax.named_scope("orthogonalize"):
        mine = orthogonalize(matrix, math.sqrt(whole_rows))
    with jax.named_scope("return_rows"):
        arrived = lax.all_to_all(mine.reshape(devices, rows, cols), both, 0, 0, tiled=True)
    with jax.named_scope("owned"):
        owned = begin(table, [mine, *(lax.ppermute(mine, "dp", step) for step in chip_steps())])

    def with_left(owned, arrived):
        plane, dp = lax.axis_index("owner"), lax.axis_index("dp")
        slots = []
        for slot in range(CAP):
            matrix = lax.all_to_all(left_rows(table, arrived, planes, slot), both, 0, 0, tiled=True)
            slots.append(jnp.where(table[OWNED + plane, dp] > slot, matrix.reshape(whole_rows, cols), 0))
        return jnp.stack(slots)

    with jax.named_scope("left"):
        owned = lax.cond(table[LEFT, 0] > 0, with_left, lambda owned, arrived: owned, owned, arrived)
    with jax.named_scope("finish"):
        update, owned = finish(lists, arrived, owned, mats)
    return new_momentum, update, owned[:, None]


def solution(mesh):
    in_specs = (P(None, ("dp", "owner"), None), P(None, ("dp", "owner"), None), P())
    out_specs = (
        P(None, ("dp", "owner"), None),
        P(None, ("dp", "owner"), None),
        P(None, ("dp", "owner"), None, None),
    )
    return jax.shard_map(shards, mesh=mesh, in_specs=in_specs, out_specs=out_specs, check_vma=False)
```

```python
import functools
import math

import jax
import jax.numpy as jnp
from jax import lax
from jax.experimental import pallas as pl
from jax.experimental.pallas import tpu as pltpu
from jax.sharding import PartitionSpec as P

ITERS = 2
CAP = 2

momentum_decay = 0.95
quintic_one = 3.4445
quintic_two = -4.775
quintic_three = 2.0315
norm_epsilon = 1e-07

HOSTS, WAYS, WORK, OWNED, LEFT = 0, 16, 32, 40, 48
PLANES, COLUMNS, TABLE_ROWS = 8, 128, 56
HOST, MATRIX, LIST_ROWS = 0, 1, 8
FAR, ROUNDS = 63, 20


def chip_steps():
    steps = ([], [], [])
    for x in range(4):
        for y in range(4):
            for core, way in ((0, 1), (1, -1)):
                here = (x * 4 + y) * 2 + core
                steps[0].append((here, here + way))
                steps[1].append((here, ((x + way) % 4 * 4 + y) * 2 + core))
                steps[2].append((here, (x * 4 + (y + way) % 4) * 2 + core))
    return steps


def neighbours():
    lane = lax.broadcasted_iota(jnp.int32, (PLANES, COLUMNS), 1)
    core, y = lane & 1, (lane >> 1) & 3

    def at(values, way):
        return pltpu.roll(values, (COLUMNS - way) % COLUMNS, 1)

    def flip(values):
        return jnp.where(core == 0, at(values, 1), at(values, -1))

    def along_x(values, sign):
        return jnp.where(core == 0, at(values, 8 * sign), at(values, -8 * sign))

    def along_y(values, sign):
        up = jnp.where(y == 3, at(values, -6), at(values, 2))
        down = jnp.where(y == 0, at(values, 6), at(values, -2))
        return jnp.where((core == 0) == (sign > 0), up, down)

    pull = (flip, lambda values: along_x(values, -1), lambda values: along_y(values, -1))
    push = (flip, lambda values: along_x(values, 1), lambda values: along_y(values, 1))
    return pull, push


def search_turn(work, label, waiting):
    pull, push = neighbours()
    best, choice = jnp.full_like(work, FAR), jnp.zeros_like(work)
    for k in range(3):
        there = pull[k](label * 8 + work + 1)
        value = jnp.where((there & 7) == k + 2, FAR, there >> 3)
        choice = jnp.where(value < best, k + 1, choice)
        best = jnp.minimum(value, best)
    message = best * 8 + jnp.where(waiting > 0, choice, 0)
    moved = jnp.where(work == 0, best + 1, 0)
    taken = jnp.zeros_like(work)
    for k in range(3):
        there = push[k](message)
        moved = jnp.where(work == k + 1, (there >> 3) + 1, moved)
        taken = jnp.where((taken == 0) & ((there & 7) == k + 1), k + 1, taken)
    label = jnp.minimum(jnp.maximum(label, moved), FAR)
    waiting = waiting + jnp.where((taken > 0) & (work == 0), 1, 0)
    for k in range(3):
        waiting = waiting + pull[k](jnp.where((taken > 0) & (work == k + 1), 1, 0) - jnp.where(taken == k + 1, 1, 0))
    return jnp.where(taken > 0, taken, work), label, waiting


def search_rest(work, label, waiting):
    def going(state):
        count, _, _, _, left = state
        return (count < ROUNDS) & (left > 0)

    def turn(state):
        count, *found, _ = state
        found = search_turn(*search_turn(*found))
        return count + 2, *found, jnp.sum(found[2])

    _, work, _, _, left = lax.while_loop(going, turn, (jnp.int32(0), work, label, waiting, jnp.sum(waiting)))
    return work, left


def iota(rows, cols, axis):
    return lax.broadcasted_iota(jnp.int32, (rows, cols), axis)


def column(row):
    n = row.shape[1]
    return jnp.sum(jnp.where(iota(n, n, 0) == iota(n, n, 1), row, 0.0), axis=1, keepdims=True)


def count_owned(planes, owner_col):
    mats = owner_col.shape[0]
    owned = jnp.zeros((PLANES, COLUMNS), jnp.float32)
    index = (iota(mats, COLUMNS, 1) & 31) * planes
    for p in range(planes):
        hits = jnp.sum(jnp.where(owner_col == index + p, 1.0, 0.0), axis=0, keepdims=True)
        owned = jnp.where(iota(PLANES, COLUMNS, 0) == p, hits, owned)
    return owned.astype(jnp.int32)


def rank_of(owner_row, owner_col):
    mats = owner_col.shape[0]
    earlier = (owner_col == owner_row) & (iota(mats, mats, 1) < iota(mats, mats, 0))
    return jnp.sum(jnp.where(earlier, 1.0, 0.0), axis=1, keepdims=True).astype(jnp.int32)


def fill_lists(planes, owner_col, rank_col, table_ref, lists_ref):
    mats, devices = owner_col.shape[0], lists_ref.shape[1]
    shift = planes.bit_length() - 1
    at_dp = jnp.where(iota(mats, COLUMNS, 1) == owner_col >> shift, 1.0, 0.0)
    hosts = table_ref[HOSTS : HOSTS + CAP * PLANES, :].astype(jnp.float32)
    found = lax.dot_general(at_dp, hosts, (((1,), (1,)), ((), ())), preferred_element_type=jnp.float32)
    wanted = iota(mats, CAP * PLANES, 1) == rank_col * PLANES + (owner_col & (planes - 1))
    host_col = jnp.sum(jnp.where(wanted, found, 0.0), axis=1, keepdims=True)
    host_row = jnp.sum(jnp.where(iota(mats, mats, 0) == iota(mats, mats, 1), host_col, 0.0), axis=0, keepdims=True)
    here = host_col.astype(jnp.int32) == iota(mats, devices, 1)
    number = (iota(mats, devices, 0) + 1).astype(jnp.float32)
    matrix_row = jnp.sum(jnp.where(here, number, 0.0), axis=0, keepdims=True) - 1.0
    lists_ref[...] = jnp.zeros_like(lists_ref)
    lists_ref[HOST : HOST + 1, :mats] = host_row.astype(jnp.int32)
    lists_ref[MATRIX : MATRIX + 1, :] = matrix_row.astype(jnp.int32)


def fill_table(planes, owned, work, left, table_ref):
    plane, lane = (iota(PLANES, COLUMNS, axis) for axis in (0, 1))
    pull, _ = neighbours()
    device = (lane & 31) * planes + plane
    none = jnp.full_like(owned, -1)
    hosts, ways = [none, none], [none, none]
    options = [(work == 0, device, 0)] + [(pull[k](work) == k + 1, pull[k](device), k + 1) for k in range(3)]
    for chosen, host, way in options:
        for slot in (1, 0):
            free = hosts[slot] < 0 if slot == 0 else (hosts[1] < 0) & (hosts[0] >= 0)
            hosts[slot] = jnp.where(chosen & free, host, hosts[slot])
            ways[slot] = jnp.where(chosen & free, way, ways[slot])
    for slot in range(CAP):
        table_ref[HOSTS + slot * PLANES : HOSTS + (slot + 1) * PLANES, :] = hosts[slot]
        table_ref[WAYS + slot * PLANES : WAYS + (slot + 1) * PLANES, :] = ways[slot]
    table_ref[WORK : WORK + PLANES, :] = work
    table_ref[OWNED : OWNED + PLANES, :] = owned
    table_ref[LEFT : LEFT + PLANES, :] = jnp.zeros_like(owned) + left


def place_left(planes, devices, table_ref):
    shift = planes.bit_length() - 1

    def each(i, idle):
        device = i // CAP
        plane, dp = device & (planes - 1), device >> shift
        host_row = HOSTS + (i % CAP) * PLANES + plane
        alone = (table_ref[OWNED + plane, dp] > i % CAP) & (table_ref[host_row, dp] < 0)

        def find(at):
            return lax.while_loop(lambda at: table_ref[WORK + (at & (planes - 1)), at >> shift] >= 0, lambda at: at + 1, at)

        @pl.when(alone)
        def _():
            table_ref[host_row, dp] = find(idle)

        return lax.cond(alone, lambda: find(idle) + 1, lambda: idle)

    lax.fori_loop(0, CAP * devices, each, jnp.int32(0))


def start_kernel(
    planes, owner_ref, momentum_ref, grad_ref, table_ref, lists_ref, new_ref, out_ref,
    new, grad, fixed, hosts, in_sem, out_sem, table_sem, rows_sem
):
    chunks = in_sem.shape[1]
    block = new.shape[0] // chunks

    def part(chunk):
        return pl.ds(chunk * block, block)

    def copies_in(chunk):
        return (
            pltpu.make_async_copy(momentum_ref.at[part(chunk)], new.at[part(chunk)], in_sem.at[0, chunk]),
            pltpu.make_async_copy(grad_ref.at[part(chunk)], grad.at[part(chunk)], in_sem.at[1, chunk]),
        )

    def copy_out(chunk):
        return pltpu.make_async_copy(new.at[part(chunk)], new_ref.at[part(chunk)], out_sem.at[chunk])

    for chunk in range(chunks):
        for copy in copies_in(chunk):
            copy.start()
    owner_row = owner_ref[...]
    owner_col = column(owner_row.astype(jnp.float32)).astype(jnp.int32)
    owned = count_owned(planes, owner_col)
    rank_col = rank_of(owner_row, owner_col)

    def each_chunk(chunk, found):
        for copy in copies_in(chunk):
            copy.wait()
        for i in range(block):
            mat = chunk * block + i
            value = grad[mat].astype(jnp.float32)
            result = momentum_decay * new[mat] + value
            new[mat] = result
            grad[mat] = (value + momentum_decay * result).astype(grad.dtype)
        copy_out(chunk).start()
        return search_turn(*found)

    found = (jnp.where(owned > 0, 0, -1), jnp.where(owned > 0, 1, 0), jnp.maximum(owned - 1, 0))
    work, left = search_rest(*lax.fori_loop(0, chunks, each_chunk, found))
    fill_table(planes, owned, work, left, table_ref)

    @pl.when(left > 0)
    def _():
        copy = pltpu.make_async_copy(table_ref, fixed, table_sem)
        copy.start()
        copy.wait()
        place_left(planes, out_ref.shape[0], fixed)
        copy = pltpu.make_async_copy(fixed, table_ref, table_sem)
        copy.start()
        copy.wait()

    fill_lists(planes, owner_col, rank_col, table_ref, lists_ref)
    copy = pltpu.make_async_copy(lists_ref, hosts, table_sem)
    copy.start()
    copy.wait()

    def each(mat, _):
        pltpu.make_async_copy(grad.at[mat], out_ref.at[hosts[HOST, mat]], rows_sem).start()

    mats = new.shape[0]
    lax.fori_loop(0, mats, each, None, unroll=8 if mats % 8 == 0 else 1)
    pltpu.make_async_copy(grad, out_ref.at[pl.ds(0, mats)], rows_sem).wait()
    for chunk in range(chunks):
        copy_out(chunk).wait()


def start(owner_table, momentum, grad, planes, devices, chunks=6):
    mats, rows, cols = momentum.shape
    while mats % chunks:
        chunks -= 1
    hbm = pl.BlockSpec(memory_space=pltpu.HBM)
    outgoing = (devices, rows, cols)
    return pl.pallas_call(
        functools.partial(start_kernel, planes),
        grid=(1,),
        in_specs=[pl.BlockSpec((1, mats), lambda *_: (0, 0)), hbm, hbm],
        out_specs=[
            pl.BlockSpec((TABLE_ROWS, COLUMNS), lambda *_: (0, 0)),
            pl.BlockSpec((LIST_ROWS, devices), lambda *_: (0, 0)),
            hbm,
            hbm,
        ],
        scratch_shapes=[
            pltpu.VMEM(momentum.shape, momentum.dtype),
            pltpu.VMEM(grad.shape, grad.dtype),
            pltpu.SMEM((TABLE_ROWS, COLUMNS), jnp.int32),
            pltpu.SMEM((LIST_ROWS, devices), jnp.int32),
            pltpu.SemaphoreType.DMA((2, chunks)),
            pltpu.SemaphoreType.DMA((chunks,)),
            pltpu.SemaphoreType.DMA,
            pltpu.SemaphoreType.DMA,
        ],
        out_shape=[
            jax.ShapeDtypeStruct((TABLE_ROWS, COLUMNS), jnp.int32),
            jax.ShapeDtypeStruct((LIST_ROWS, devices), jnp.int32),
            jax.ShapeDtypeStruct(momentum.shape, jnp.float32),
            jax.ShapeDtypeStruct(outgoing, jnp.bfloat16),
        ],
        compiler_params=pltpu.CompilerParams(vmem_limit_bytes=60 * 1024 * 1024),
        name="start",
    )(owner_table.reshape(1, mats), momentum, grad)


def orthogonalize_kernel(scale, x_ref, out_ref, iterate_ref, gram_ref, poly_ref):
    rows, cols = x_ref.shape
    tile, side = min(256, rows), min(256, cols) if cols % 256 == 0 else 128
    f32, bf16 = jnp.float32, jnp.bfloat16
    starts = range(0, cols, side)

    def put(ref, i, block):
        ref[i : i + side, i:] = block
        for j in range(i + side, cols, side):
            ref[j : j + side, i : i + side] = block[:, j - i : j - i + side].T

    def gram_rows(ref, i):
        return lax.dot_general(ref[:, i : i + side], ref[:, i:], (((0,), (0,)), ((), ())), preferred_element_type=f32)

    def poly():
        for i in starts:
            square = jnp.dot(gram_ref[i : i + side, :], gram_ref[:, i:], preferred_element_type=f32)
            put(poly_ref, i, (quintic_two * gram_ref[i : i + side, i:].astype(f32) + quintic_three * square).astype(bf16))

    def apply(source_ref, target_ref, factor, last):
        for i in range(0, rows, tile):
            part = source_ref[i : i + tile, :]
            step = quintic_one * part.astype(f32) + jnp.dot(part, poly_ref[...], preferred_element_type=f32)
            step = (step * factor).astype(bf16) if factor is not None else step.astype(bf16)
            step = step * jnp.asarray(scale, bf16) if last else step
            target_ref[i : i + tile, :] = step

    gram = [gram_rows(x_ref, i) for i in starts]
    diagonal = lax.broadcasted_iota(jnp.int32, (side, side), 0) == lax.broadcasted_iota(jnp.int32, (side, side), 1)
    squares = sum(jnp.where(diagonal, block[:, :side], 0.0) for block in gram)
    trace = jnp.sum(jnp.sum(squares, axis=0, keepdims=True), axis=1, keepdims=True)
    factor = 1.0 / (jnp.sqrt(trace) + norm_epsilon)
    for i, block in zip(starts, gram):
        put(gram_ref, i, (block * factor * factor).astype(bf16))
    poly()
    apply(x_ref, iterate_ref, factor, False)
    for step in range(1, ITERS):
        for i in starts:
            put(gram_ref, i, gram_rows(iterate_ref, i).astype(bf16))
        poly()
        apply(iterate_ref, out_ref, None, True)


def orthogonalize(matrix, scale):
    rows, cols = matrix.shape
    return pl.pallas_call(
        functools.partial(orthogonalize_kernel, scale),
        out_shape=jax.ShapeDtypeStruct((rows, cols), jnp.bfloat16),
        scratch_shapes=[
            pltpu.VMEM((rows, cols), jnp.bfloat16),
            pltpu.VMEM((cols, cols), jnp.bfloat16),
            pltpu.VMEM((cols, cols), jnp.bfloat16),
        ],
        compiler_params=pltpu.CompilerParams(vmem_limit_bytes=24 * 1024 * 1024),
        cost_estimate=pl.CostEstimate(flops=ITERS * 2 * cols * cols * (2 * rows + cols), bytes_accessed=4 * rows * cols, transcendentals=0),
        name="orthogonalize",
    )(matrix)


def begin_kernel(table_ref, lists_ref, mine_ref, owned_ref, again_ref, held_ref, zero_ref, in_sem, out_sem):
    again_ref[...] = lists_ref[...]
    plane, dp = lax.axis_index("owner"), lax.axis_index("dp")
    ways = [table_ref[WAYS + slot * PLANES + plane, dp] for slot in range(CAP)]
    bring = pltpu.make_async_copy(mine_ref, held_ref, in_sem)
    bring.start()
    zero_ref[...] = jnp.zeros_like(zero_ref)
    tile = zero_ref.shape[0]

    def zeros(act):
        for slot, way in enumerate(ways):

            @pl.when(way < 0)
            def _():
                for i in range(owned_ref.shape[1] // tile):
                    act(pltpu.make_async_copy(zero_ref, owned_ref.at[slot, pl.ds(i * tile, tile)], out_sem.at[slot, i]))

    def own(act):
        for slot, way in enumerate(ways):

            @pl.when(way == 0)
            def _():
                act(pltpu.make_async_copy(held_ref, owned_ref.at[slot], out_sem.at[slot, 0]))

    zeros(lambda copy: copy.start())
    bring.wait()
    own(lambda copy: copy.start())
    zeros(lambda copy: copy.wait())
    own(lambda copy: copy.wait())


def begin(table, lists, mine):
    hbm = pl.BlockSpec(memory_space=pltpu.HBM)
    rows, cols = mine.shape
    tile = min(256, rows)
    return pl.pallas_call(
        begin_kernel,
        grid_spec=pltpu.PrefetchScalarGridSpec(
            num_scalar_prefetch=1,
            grid=(1,),
            in_specs=[pl.BlockSpec(lists.shape, lambda *_: (0, 0)), hbm],
            out_specs=[hbm, pl.BlockSpec(lists.shape, lambda *_: (0, 0))],
            scratch_shapes=[
                pltpu.VMEM((rows, cols), mine.dtype),
                pltpu.VMEM((tile, cols), mine.dtype),
                pltpu.SemaphoreType.DMA,
                pltpu.SemaphoreType.DMA((CAP, rows // tile)),
            ],
        ),
        out_shape=[
            jax.ShapeDtypeStruct((CAP, rows, cols), mine.dtype),
            jax.ShapeDtypeStruct(lists.shape, lists.dtype),
        ],
        compiler_params=pltpu.CompilerParams(vmem_limit_bytes=8 * 1024 * 1024),
        cost_estimate=pl.CostEstimate(flops=0, bytes_accessed=6 * rows * cols, transcendentals=0),
        name="begin",
    )(table, lists, mine)


def receive_kernel(table_ref, *refs):
    sources, (_, owned_ref, held_ref, in_sem, out_sem) = refs[:-5], refs[-5:]
    plane, dp = lax.axis_index("owner"), lax.axis_index("dp")
    parts = in_sem.shape[1]
    rows = held_ref.shape[1] // parts
    steps = [(slot, part) for slot in range(CAP) for part in range(parts)]
    ways = [table_ref[WAYS + slot * PLANES + plane, dp] for slot in range(CAP)]

    def bring(slot, part, act):
        span = pl.ds(part * rows, rows)
        for k, source in enumerate(sources):

            @pl.when(ways[slot] == k + 1)
            def _():
                act(pltpu.make_async_copy(source.at[span], held_ref.at[slot, span], in_sem.at[slot, part]))

    def put(slot, part, act):
        span = pl.ds(part * rows, rows)

        @pl.when(ways[slot] > 0)
        def _():
            act(pltpu.make_async_copy(held_ref.at[slot, span], owned_ref.at[slot, span], out_sem.at[slot, part]))

    for step in steps:
        bring(*step, lambda copy: copy.start())
    for step in steps:
        bring(*step, lambda copy: copy.wait())
        put(*step, lambda copy: copy.start())
    for step in steps:
        put(*step, lambda copy: copy.wait())


def receive(table, sources, owned):
    hbm = pl.BlockSpec(memory_space=pltpu.HBM)
    parts = 4
    return pl.pallas_call(
        receive_kernel,
        grid_spec=pltpu.PrefetchScalarGridSpec(
            num_scalar_prefetch=1,
            grid=(1,),
            in_specs=[hbm] * (len(sources) + 1),
            out_specs=hbm,
            scratch_shapes=[
                pltpu.VMEM(owned.shape, owned.dtype),
                pltpu.SemaphoreType.DMA((CAP, parts)),
                pltpu.SemaphoreType.DMA((CAP, parts)),
            ],
        ),
        out_shape=jax.ShapeDtypeStruct(owned.shape, owned.dtype),
        input_output_aliases={1 + len(sources): 0},
        compiler_params=pltpu.CompilerParams(vmem_limit_bytes=8 * 1024 * 1024),
        name="receive",
    )(table, *sources, owned)


def finish_kernel(lists_ref, rows_ref, _, update_ref, owned_ref, staged_ref, sem):
    devices = rows_ref.shape[0]
    count = min(32, devices)

    def each(chunk, _):
        first = chunk * count
        staged_ref[pl.ds(first, count)] = rows_ref[pl.ds(first, count)].astype(jnp.float32)
        for i in range(count):
            matrix = lists_ref[MATRIX, first + i]

            @pl.when(matrix >= 0)
            def _():
                pltpu.make_async_copy(staged_ref.at[first + i], update_ref.at[matrix], sem).start()

    lax.fori_loop(0, devices // count, each, None)
    pltpu.make_async_copy(staged_ref.at[pl.ds(0, update_ref.shape[0])], update_ref, sem).wait()


def finish(lists, arrived, owned, mats):
    hbm = pl.BlockSpec(memory_space=pltpu.HBM)
    _, rows, cols = arrived.shape
    return pl.pallas_call(
        finish_kernel,
        grid_spec=pltpu.PrefetchScalarGridSpec(
            num_scalar_prefetch=1,
            grid=(1,),
            in_specs=[pl.BlockSpec(arrived.shape, lambda *_: (0, 0, 0)), hbm],
            out_specs=[hbm, hbm],
            scratch_shapes=[pltpu.VMEM(arrived.shape, jnp.float32), pltpu.SemaphoreType.DMA],
        ),
        out_shape=[
            jax.ShapeDtypeStruct((mats, rows, cols), jnp.float32),
            jax.ShapeDtypeStruct(owned.shape, owned.dtype),
        ],
        input_output_aliases={2: 1},
        compiler_params=pltpu.CompilerParams(vmem_limit_bytes=20 * 1024 * 1024),
        name="finish",
    )(lists, arrived, owned)


def left_kernel(planes, slot, table_ref, arrived_ref, out_ref):
    shift = planes.bit_length() - 1

    def each(i, _):
        host = table_ref[HOSTS + slot * PLANES + (i & (planes - 1)), i >> shift]
        out_ref[i] = arrived_ref[jnp.maximum(host, 0)]

    lax.fori_loop(0, out_ref.shape[0], each, None)


def left_rows(table, arrived, planes, slot):
    whole = pl.BlockSpec(arrived.shape, lambda *_: (0, 0, 0))
    return pl.pallas_call(
        functools.partial(left_kernel, planes, slot),
        grid_spec=pltpu.PrefetchScalarGridSpec(num_scalar_prefetch=1, grid=(1,), in_specs=[whole], out_specs=whole),
        out_shape=jax.ShapeDtypeStruct(arrived.shape, arrived.dtype),
        compiler_params=pltpu.CompilerParams(vmem_limit_bytes=14 * 1024 * 1024),
        name="left",
    )(table, arrived)


def shards(momentum, grad, owner_table):
    dp_count = lax.axis_size("dp")
    planes = lax.axis_size("owner")
    devices = dp_count * planes
    mats, rows, cols = momentum.shape
    whole_rows = devices * rows
    both = ("dp", "owner")
    with jax.named_scope("start"):
        table, lists, new_momentum, outgoing = start(owner_table, momentum, grad, planes, devices)
    with jax.named_scope("gather_matrix"):
        received = lax.all_to_all(outgoing, both, 0, 0, tiled=True)
        matrix = received.reshape(whole_rows, cols)
    with jax.named_scope("orthogonalize"):
        mine = orthogonalize(matrix, math.sqrt(whole_rows))
    with jax.named_scope("return_rows"):
        arrived = lax.all_to_all(mine.reshape(devices, rows, cols), both, 0, 0, tiled=True)
    with jax.named_scope("owned"):
        sources = [lax.ppermute(mine, "dp", step) for step in chip_steps()]
        owned, lists = begin(table, lists, mine)
        owned = receive(table, sources, owned)

    def with_left(owned, arrived):
        plane, dp = lax.axis_index("owner"), lax.axis_index("dp")
        slots = []
        for slot in range(CAP):
            matrix = lax.all_to_all(left_rows(table, arrived, planes, slot), both, 0, 0, tiled=True)
            slots.append(jnp.where(table[OWNED + plane, dp] > slot, matrix.reshape(whole_rows, cols), 0))
        return jnp.stack(slots)

    with jax.named_scope("left"):
        owned = lax.cond(table[LEFT, 0] > 0, with_left, lambda owned, arrived: owned, owned, arrived)
    with jax.named_scope("finish"):
        update, owned = finish(lists, arrived, owned, mats)
    return new_momentum, update, owned[:, None]


def solution(mesh):
    in_specs = (P(None, ("dp", "owner"), None), P(None, ("dp", "owner"), None), P())
    out_specs = (
        P(None, ("dp", "owner"), None),
        P(None, ("dp", "owner"), None),
        P(None, ("dp", "owner"), None, None),
    )
    return jax.shard_map(shards, mesh=mesh, in_specs=in_specs, out_specs=out_specs, check_vma=False)
```
